128 devices in a mesh: gas: 64 (over y, x, z), grp: 2 (over core).
Axes of the slice: x: 4, y: 4, z: 4, core: 2. Of those that a mesh axis runs over, the one named last changes fastest.
Arguments:
- gas_state: float32 [6, 256, 64, 256], P(None, 'gas', 'grp')
- particle_blocks: float32 [5, 131072, 128], P(None, ('gas', 'grp'))
- owner: int32 [131072, 1], P(('gas', 'grp')), may hold values from 0 to 127; in each aligned block of 1024 rows (0 to 1023, 1024 to 2047, ...) at most 16 rows name the same one
- host_cell: int32 [131072], P(('gas', 'grp')), may hold values from 0 to 32767
- live_count: int32 [131072], P(('gas', 'grp')), may hold values from 1 to 128, as said below
Outputs:
- gas_next: float32 [6, 256, 64, 256], P(None, 'gas', 'grp')
- parcels_next: float32 [5, 131072, 128], P(None, ('gas', 'grp'))
The draws below stay inside these ranges and needn't reach their ends.
Inputs may be any that keep to these rules, and one draw needn't show every extreme that they name: Among the blocks of one device, at most 16 name the same owner. `live_count`: the first block of every device is full.
All inputs are finite; a program needn't handle non-finite values.
Results may differ from the reference program's by a relative error of at most 0.00002.
Values sent between devices are 32-bit elements; how exact they have to be, the bound alone decides.
No kernel may reach another device: no remote copies, remote signals or barrier semaphores. Data moves between devices by JAX's collectives and lax.ppermute only.
A program may use at most 128 MiB of HBM per device.

```python
import math
import jax
import jax.numpy as jnp
import numpy as np
from jax import lax

CX = 4
CY = 32
NZ = 256
BLK_DEV = 1024
PSLOT = 128
NSUB = 4
NX = 256
NY = 64
CELLS_DEV = 32768
BLOCKS = 131072
CAP = 16
N_GRP = 2
DEVICES = 128


def draw_gas_state(key, part):
    key = jax.random.fold_in(key, 11)
    stochastic_seeds = jax.random.split(key, 4)
    grid_extent = (NX, NY, NZ)
    specific_volume_inverse = 1.0 + 0.15 * jax.random.truncated_normal(stochastic_seeds[0], -2.0, 2.0, grid_extent, jnp.float32)
    particle_motion = 0.3 * jax.random.truncated_normal(stochastic_seeds[1], -2.5, 2.5, (3,) + grid_extent, jnp.float32)
    particle_thermal = 1.0 + 0.15 * jax.random.truncated_normal(stochastic_seeds[2], -2.0, 2.0, grid_extent, jnp.float32)
    vapor_share = jax.random.uniform(stochastic_seeds[3], grid_extent, jnp.float32, 0.0, 0.2)
    layered_tensors = jnp.concatenate([specific_volume_inverse[None], specific_volume_inverse[None] * particle_motion, (specific_volume_inverse * particle_thermal)[None], (specific_volume_inverse * vapor_share)[None]], axis=0)
    return layered_tensors.astype(jnp.float32)


def draw_particle_blocks(key, part):
    key = jax.random.fold_in(key, 12)
    stochastic_seeds = jax.random.split(key, 3)
    grid_extent = (BLOCKS, PSLOT)
    particle_weight = jnp.exp(jax.random.uniform(stochastic_seeds[0], grid_extent, jnp.float32, jnp.log(0.5), jnp.log(2.0)))
    bulk_motion_magnitude = 0.5 * jax.random.truncated_normal(stochastic_seeds[1], -2.0, 2.0, (3,) + grid_extent, jnp.float32)
    particle_thermal = jax.random.uniform(stochastic_seeds[2], grid_extent, jnp.float32, 0.4, 0.9)
    return jnp.concatenate([particle_weight[None], bulk_motion_magnitude, particle_thermal[None]], axis=0).astype(jnp.float32)


def draw_live_count(key, part):
    key = jax.random.fold_in(key, 13)
    counts = jax.random.randint(key, (BLOCKS,), PSLOT // 8, PSLOT + PSLOT // 4 + 1)
    counts = jnp.minimum(counts, PSLOT)
    first = jnp.arange(BLOCKS) % BLK_DEV == 0
    return jnp.where(first, PSLOT, counts).astype(jnp.int32)


def set_ends(result, key, least, largest):
    longest = result.shape.index(max(result.shape))
    spots = []
    for shift in (0, 1):
        where = [jax.random.randint(jax.random.fold_in(key, axis), (), 0, length) for axis, length in enumerate(result.shape)]
        where[longest] = (where[longest] + shift) % result.shape[longest]
        spots.append(tuple(where))
    return result.at[spots[0]].set(least).at[spots[1]].set(largest)


def routed_block(own_key, own, number, rows, count, top, limit, skew):
    sequence = jax.random.permutation(own_key, count)
    packed, ordinary = shares(count, rows * top, limit, skew, True), shares(count, rows * top, limit, skew, False)
    places = jnp.arange(count)

    def named(tallies, rotation):
        used = int((tallies > 0).sum())
        fixed = max(1, used // 4)
        moved = fixed + (places - fixed + rotation * (used - fixed)) % max(1, count - fixed)
        return jnp.zeros((count,), jnp.int32).at[sequence[jnp.where(places < fixed, places, moved)]].set(jnp.asarray(tallies, jnp.int32))

    tallies = jnp.where(number % 4 == 0, named(packed, number // 4), named(ordinary, number - number // 4 - 1))
    mixed = jax.random.permutation(jax.random.fold_in(own, 3), count)
    giver, sink = mixed[0:count // 2 * 2:2], mixed[1:count // 2 * 2:2]
    margin = jnp.minimum(tallies[giver] - 1, limit - tallies[sink]) // 2
    margin = jnp.where((giver == sequence[0]) | (sink == sequence[0]) | (tallies[sink] == 0), 0, jnp.maximum(margin, 0))
    moved = jax.random.randint(jax.random.fold_in(own, 4), (count // 2,), 0, 1 << 20) % (margin + 1)
    tallies = tallies.at[giver].add(-moved).at[sink].add(moved)
    items = jnp.searchsorted(jnp.cumsum(tallies), jnp.arange(rows * top), side="right").astype(jnp.int32)
    table = items.reshape(top, rows).T
    table = table[jax.random.permutation(jax.random.fold_in(own, 1), rows)]
    rotation = jax.random.randint(jax.random.fold_in(own, 2), (rows, 1), 0, top)
    return jnp.take_along_axis(table, (jnp.arange(top)[None, :] + rotation) % top, axis=1)


def shares(number_of, total, limit, skew, full):
    loads = [(1 << 20) // math.isqrt(standing ** skew) + 1 for standing in range(1, number_of + 1)]
    largest = limit if full else min(limit, max(-(-total // number_of), total * loads[0] // sum(loads)))
    least = 1 if total - largest >= number_of - 1 else 0
    given, rest = [largest] + [least] * (number_of - 1), total - largest - least * (number_of - 1)
    while rest > 0:
        movable = [i for i in range(1, number_of) if given[i] < largest] or [i for i in range(1, number_of) if given[i] < limit]
        mass, budget = sum([loads[i] for i in movable]), rest
        for i in movable:
            addition = min(limit - given[i], max(1, budget * loads[i] // mass), rest)
            given[i] = given[i] + addition
            rest = rest - addition
    return np.array(given)


def setup_inputs(seed: int = 0) -> dict:
    keys = jax.random.split(jax.random.key(seed), 6)
    gas_state = draw_gas_state(jax.random.fold_in(keys[5], 71), 0)
    particle_blocks = draw_particle_blocks(jax.random.fold_in(keys[5], 71), 0)
    owner_keys = jax.random.split(jax.random.fold_in(keys[2], 1), BLOCKS // BLK_DEV)
    owner_turns = jax.random.permutation(jax.random.fold_in(keys[2], 3), BLOCKS // BLK_DEV)
    owner = jax.vmap(lambda own, number: routed_block(jax.random.fold_in(keys[2], 2), own, number, BLK_DEV, DEVICES, 1, CAP, 2))(owner_keys, owner_turns).reshape((BLOCKS, 1))
    host_cell = set_ends(jax.random.randint(keys[3], (BLOCKS,), 0, CELLS_DEV), jax.random.fold_in(keys[3], 1), 0, CELLS_DEV - 1).astype(jnp.int32)
    live_count = draw_live_count(jax.random.fold_in(keys[5], 71), 0)
    return dict(gas_state=gas_state, particle_blocks=particle_blocks, owner=owner, host_cell=host_cell, live_count=live_count)


LAM = 0.1
GAMMA_ADIABATIC = 1.4
CLOCK_INCREMENT = 0.25
TAU_DRAG = 0.8
THERMAL_RELAX = 1.2
EVAP_RATE = 0.5
LATENT_EVAPORATE = 0.3
WEIGHT = 0.05

def physical(present_solution, d):
    specific_volume_inverse = present_solution[0]
    particle_motion = present_solution[1 + d] / specific_volume_inverse
    particle_thermal = present_solution[4] / specific_volume_inverse
    fluxes = present_solution * particle_motion[None]
    fluxes = fluxes.at[1 + d].add(present_solution[4])
    signal_propagation_rates = jnp.abs(particle_motion) + jnp.sqrt(GAMMA_ADIABATIC * particle_thermal)
    return (fluxes, signal_propagation_rates)

def divergence(padded):
    padded = jnp.concatenate([padded[:, :, :, :1], padded, padded[:, :, :, -1:]], axis=3)
    summed = None
    for d in range(3):
        cuts = [slice(None)]
        for e in range(3):
            cuts.append(slice(None) if e == d else slice(1, padded.shape[1 + e] - 1))
        inner = padded[tuple(cuts)]
        fluxes, signal_propagation_rates = physical(inner, d)
        count = inner.shape[1 + d]
        lower_f = lax.slice_in_dim(fluxes, 0, count - 1, axis=1 + d)
        upper_f = lax.slice_in_dim(fluxes, 1, count, axis=1 + d)
        lower_q = lax.slice_in_dim(inner, 0, count - 1, axis=1 + d)
        upper_q = lax.slice_in_dim(inner, 1, count, axis=1 + d)
        speeds = jnp.maximum(lax.slice_in_dim(signal_propagation_rates, 0, count - 1, axis=d), lax.slice_in_dim(signal_propagation_rates, 1, count, axis=d))
        face_flux = 0.5 * (lower_f + upper_f) - 0.5 * speeds[None] * (upper_q - lower_q)
        term = lax.slice_in_dim(face_flux, 1, count - 1, axis=1 + d) - lax.slice_in_dim(face_flux, 0, count - 2, axis=1 + d)
        summed = term if summed is None else summed + term
    return summed

def integrate(particle_blocks, solution_history, live_count):
    gas_speed = (solution_history[1:4] / solution_history[0][None])[:, :, None]
    ambient_thermal = (solution_history[4] / solution_history[0])[:, None]
    vapor_share = (solution_history[5] / solution_history[0])[:, None]
    particle_weight = particle_blocks[0]
    bulk_motion_magnitude = particle_blocks[1:4]
    particle_thermal = particle_blocks[4]
    for substep in range(NSUB):
        surface_extent_power = jnp.exp(2.0 / 3.0 * jnp.log(particle_weight))
        equilibrium_vapor_share = 0.3 * particle_thermal * particle_thermal / (1.0 + particle_thermal * particle_thermal)
        revised_weight = particle_weight * jnp.exp(-CLOCK_INCREMENT * EVAP_RATE * (equilibrium_vapor_share - vapor_share) / surface_extent_power)
        bulk_motion_magnitude = bulk_motion_magnitude + (gas_speed - bulk_motion_magnitude) * (1.0 - jnp.exp(-CLOCK_INCREMENT / (TAU_DRAG * surface_extent_power)))
        particle_thermal = particle_thermal + (ambient_thermal - particle_thermal) * (1.0 - jnp.exp(-CLOCK_INCREMENT / (THERMAL_RELAX * surface_extent_power))) - LATENT_EVAPORATE * (particle_weight - revised_weight) / revised_weight
        particle_weight = revised_weight
    live = jnp.arange(particle_blocks.shape[2])[None, :] < live_count[:, None]
    ending_outcome = jnp.concatenate([particle_weight[None], bulk_motion_magnitude, particle_thermal[None]], axis=0)
    ending_outcome = jnp.where(live[None], ending_outcome, particle_blocks)
    change_mass = lax.optimization_barrier(jnp.sum(ending_outcome[0] - particle_blocks[0], axis=1))
    change_momentum = lax.optimization_barrier(jnp.sum(ending_outcome[0][None] * ending_outcome[1:4] - particle_blocks[0][None] * particle_blocks[1:4], axis=2))
    change_heat = lax.optimization_barrier(jnp.sum(ending_outcome[0] * ending_outcome[4] - particle_blocks[0] * particle_blocks[4], axis=1))
    sources = -jnp.concatenate([change_mass[None], change_momentum, change_heat[None], change_mass[None]], axis=0)
    return (ending_outcome, sources)

def edge_pad(field):
    return jnp.pad(field, ((0, 0), (1, 1), (1, 1), (0, 0)), mode='edge')

def reference(gas_state, particle_blocks, owner, host_cell, live_count):
    section_one = gas_state - LAM * divergence(edge_pad(gas_state))
    section_two = 0.75 * gas_state + 0.25 * (section_one - LAM * divergence(edge_pad(section_one)))
    section_three = gas_state / 3.0 + 2.0 / 3.0 * (section_two - LAM * divergence(edge_pad(section_two)))
    owner_row = owner[:, 0]
    gas_part = owner_row // N_GRP
    pair_part = owner_row % N_GRP
    row_x = host_cell // (CY * NZ)
    col_y = host_cell // NZ % CY
    depth = host_cell % NZ
    flat = (((gas_part * CX + row_x) * NY + pair_part * CY + col_y) * NZ + depth).astype(jnp.int32)
    flat_state = gas_state.reshape(6, -1)
    solution_history = jnp.take(flat_state, flat, axis=1)
    parcels_next, sources = integrate(particle_blocks, solution_history, live_count)
    cells = jnp.zeros(flat_state.shape, jnp.float32).at[:, flat].add(sources)
    gas_next = section_three + WEIGHT * cells.reshape(gas_state.shape)
    return (gas_next, parcels_next)
```

```python
import jax
import jax.numpy as jnp
from jax import lax
from jax.experimental import pallas as pl
from jax.experimental.pallas import tpu as pltpu
from jax.sharding import PartitionSpec as P

AXES = ("gas", "grp")
DEVICES = 128
LANES = 128
CAP = 16
CX, CY, NZ = 4, 32, 256
ROWS = CX * CY
BLK_DEV = 1024
CHUNKS = BLK_DEV // LANES
NSUB = 4
NVAR = 5
PIECES = 3
HALO = 3
EXT_X = CX + 2 * HALO
EXT_Y = CY + 8

LAM = 0.1
GAMMA_ADIABATIC = 1.4
CLOCK_INCREMENT = 0.25
TAU_DRAG = 0.8
THERMAL_RELAX = 1.2
EVAP_RATE = 0.5
LATENT_EVAPORATE = 0.3
WEIGHT = 0.05
LOG2E = 1.4426950408889634

F32 = jnp.float32
BF16 = jnp.bfloat16
VMEM_LIMIT = 48 * 1024 * 1024


def iota(shape, dim):
    return lax.broadcasted_iota(jnp.int32, shape, dim)


def dot(a, b):
    return lax.dot_general(a, b, (((1,), (0,)), ((), ())), preferred_element_type=F32)


def dot_nt(a, b):
    return lax.dot_general(a, b, (((1,), (1,)), ((), ())), preferred_element_type=F32)


def split(x):
    pieces = []
    for _ in range(PIECES):
        piece = x.astype(BF16)
        pieces.append(piece)
        x = x - piece.astype(F32)
    return pieces


def ones_where(mask):
    return jnp.where(mask, 1.0, 0.0).astype(BF16)


def compiler_params():
    return pltpu.CompilerParams(vmem_limit_bytes=VMEM_LIMIT)


def request_kernel(owner_ref, cell_ref, req_ref, rank_ref):
    down = iota((LANES, LANES), 0)
    across = iota((LANES, LANES), 1)
    earlier = ones_where(down < across)
    every = jnp.ones((LANES, LANES), BF16)
    before = jnp.zeros((LANES, LANES), F32)
    total = jnp.zeros((LANES, LANES), F32)
    for i in range(CHUNKS):
        named = down == owner_ref[i : i + 1, :]
        hot = ones_where(named)
        count = dot(hot, earlier) + before
        rank = jnp.sum(jnp.where(named, count, 0.0), axis=0, keepdims=True).astype(jnp.int32)
        rank_ref[i : i + 1, :] = rank
        cell = cell_ref[i : i + 1, :]
        high = (((cell >> 8) + 1) << 8).astype(F32)
        low = (cell & 255).astype(F32)
        placed = down == rank
        total = total + dot_nt(hot, jnp.where(placed, high, 0.0).astype(BF16))
        total = total + dot_nt(hot, jnp.where(placed, low, 0.0).astype(BF16))
        before = before + dot(hot, every)
    req_ref[...] = total.astype(jnp.int32) - 256


def table_kernel(gas_ref, table_ref):
    inverse = 1.0 / gas_ref[0]
    for c in range(NVAR):
        value = gas_ref[1 + c] * inverse
        for half in range(2):
            turned = value[:, half * LANES : (half + 1) * LANES].T
            for p, piece in enumerate(split(turned)):
                start = p * 2 * ROWS + half * ROWS
                table_ref[c * LANES : (c + 1) * LANES, start : start + ROWS] = piece


def cell_parts(asked_ref):
    cell = asked_ref[...].astype(F32).T.astype(jnp.int32)
    return (cell >> 8) + ROWS * ((cell >> 7) & 1), cell & (LANES - 1)


def gather_kernel(asked_ref, table_ref, reply_ref, found):
    row, lane = cell_parts(asked_ref)
    table = table_ref[...]
    found[...] = jnp.zeros((LANES, LANES), F32)
    for pair in range(CAP // 2):
        k = 2 * pair
        rows = jnp.concatenate([row[k : k + 1], row[k + 1 : k + 2]], axis=1)
        lanes = jnp.concatenate([lane[k : k + 1], lane[k + 1 : k + 2]], axis=1)
        hot = ones_where(iota((2 * ROWS, 2 * LANES), 0) == rows)
        values = dot(table, jnp.concatenate([hot] * PIECES, axis=0))
        here = iota((LANES, 2 * LANES), 0) == lanes
        for c in range(NVAR):
            part = values[c * LANES : (c + 1) * LANES]
            picked = jnp.sum(jnp.where(here, part, 0.0), axis=0, keepdims=True)
            found[c * CAP + k : c * CAP + k + 1, :] = picked[:, :LANES]
            found[c * CAP + k + 1 : c * CAP + k + 2, :] = picked[:, LANES:]
    reply_ref[...] = found[...].T


def integrate(parcels, gas_vars):
    mass, speeds, thermal = parcels[0], parcels[1:4], parcels[4]
    ambient, vapor = gas_vars[3], gas_vars[4]
    level = jnp.log2(mass)
    gain = jnp.zeros_like(mass)
    exposure = jnp.zeros_like(mass)
    headroom = 0.3 - vapor
    for _ in range(NSUB):
        inverse = jnp.exp2((-2.0 / 3.0) * (level + gain))
        share = headroom - 0.3 * (1.0 / (1.0 + thermal * thermal))
        loss = (CLOCK_INCREMENT * EVAP_RATE * LOG2E) * share * inverse
        kept = jnp.exp2((-CLOCK_INCREMENT / THERMAL_RELAX * LOG2E) * inverse)
        thermal = (
            ambient
            + (thermal - ambient) * kept
            - LATENT_EVAPORATE * (jnp.exp2(loss) - 1.0)
        )
        gain = gain - loss
        exposure = exposure + inverse
    drag = jnp.exp2((-CLOCK_INCREMENT / TAU_DRAG * LOG2E) * exposure)
    moved = [gas_vars[c] + (speeds[c] - gas_vars[c]) * drag for c in range(3)]
    return [mass * jnp.exp2(gain)] + moved + [thermal]


def parcel_kernel(
    owner_ref, rank_ref, live_ref, ans_ref, old_ref, new_ref, send_ref, columns, answers, spread, gather
):
    step = pl.program_id(0)
    per_step = old_ref.shape[1] // LANES

    @pl.when(step == 0)
    def _():
        pad = jnp.zeros((LANES - 3 * CHUNKS, LANES), F32)
        rows = [owner_ref[...], rank_ref[...], live_ref[...]]
        stack = jnp.concatenate([r.astype(F32) for r in rows] + [pad], axis=0)
        columns[...] = stack.T.astype(BF16)
        answers[...] = jnp.concatenate(split(ans_ref[...]), axis=1)
        shape = (PIECES * LANES, NVAR * LANES)
        spread[...] = ones_where((iota(shape, 0) % LANES) // CAP == iota(shape, 1) // LANES)
        shape = (NVAR * LANES, LANES)
        gather[...] = ones_where(iota(shape, 0) // LANES == iota(shape, 1) // CAP)
        send_ref[...] = jnp.zeros((LANES, LANES), F32)

    across = iota((LANES, LANES), 1)
    for j in range(per_step):
        i = step * per_step + j
        shape = (LANES, 3 * LANES)
        chosen = ones_where(iota(shape, 0) == i + CHUNKS * (iota(shape, 1) // LANES))
        wide = dot(columns[...], chosen).astype(jnp.int32)
        owner, rank, live = (wide[:, s * LANES : (s + 1) * LANES] for s in range(3))
        slot = across % CAP == rank
        received = dot(ones_where(owner == across), answers[...])
        mine = jnp.where(jnp.concatenate([slot] * PIECES, axis=1), received, 0.0).astype(BF16)
        gas_wide = dot(mine, spread[...])
        gas_vars = [gas_wide[:, c * LANES : (c + 1) * LANES] for c in range(NVAR)]
        here = slice(j * LANES, (j + 1) * LANES)
        old = [old_ref[c, here, :] for c in range(5)]
        alive = across < live
        new = [jnp.where(alive, n, o) for n, o in zip(integrate(old, gas_vars), old)]
        for c in range(5):
            new_ref[c, here, :] = new[c]
        change = [new[0] - old[0]] + [new[0] * new[c] - old[0] * old[c] for c in range(1, 5)]
        pieces = split(jnp.concatenate(change, axis=1))
        summed = sum(dot(piece, gather[...]) for piece in pieces)
        placed = jnp.where(slot, -summed, 0.0)
        hot = ones_where(iota((LANES, LANES), 0) == owner_ref[pl.ds(i, 1), :])
        send_ref[...] += sum(dot(hot, piece) for piece in split(placed))


def scatter_kernel(asked_ref, come_ref, section_ref, out_ref, total):
    row, lane = cell_parts(asked_ref)
    pieces = [p.astype(F32) for p in split(come_ref[...].T)]
    for pair in range(CAP // 2):
        hots, parts = [], []
        for k in (2 * pair, 2 * pair + 1):
            hot = ones_where(iota((2 * ROWS, LANES), 0) == row[k : k + 1])
            here = iota((LANES, LANES), 0) == lane[k : k + 1]
            for piece in pieces:
                hots.append(hot)
                parts.append(
                    jnp.concatenate(
                        [
                            jnp.where(here, piece[c * CAP + k : c * CAP + k + 1], 0.0)
                            for c in range(NVAR)
                        ],
                        axis=0,
                    ).astype(BF16)
                )
        added = dot_nt(jnp.concatenate(parts, axis=1), jnp.concatenate(hots, axis=1))
        if pair == 0:
            total[...] = added
        else:
            total[...] += added
    for c in range(NVAR):
        for half in range(2):
            cells = WEIGHT * total[c * LANES : (c + 1) * LANES, half * ROWS : (half + 1) * ROWS].T
            z = slice(half * LANES, (half + 1) * LANES)
            out_ref[c, :, z] = section_ref[c, :, z] + cells
            if c == 0:
                out_ref[NVAR, :, z] = section_ref[NVAR, :, z] + cells


def gas_kernel(
    place_ref, gas_ref, edge_ref, low_ref, high_ref, out_ref, q0, q1, q2, prim, face
):
    pair, first, last = place_ref[0], place_ref[1], place_ref[2]
    own = pl.ds(pl.multiple_of(pair * 8, 8), CY)
    side = pl.ds(pl.multiple_of((1 - pair) * CY, 8), 8)
    inner = slice(HALO, HALO + CX)
    q0[:, inner, own, :] = gas_ref[...]
    q0[:, inner, side, :] = edge_ref[...]
    for ref, start in ((low_ref, 0), (high_ref, HALO + CX)):
        q0[:, start : start + HALO, own, :] = ref[:, :, :CY, :]
        q0[:, start : start + HALO, side, :] = ref[:, :, CY:, :]

    def ghosts(q):
        @pl.when(first == 1)
        def _():
            q[:, HALO - 1] = q[:, HALO]

        @pl.when(last == 1)
        def _():
            q[:, HALO + CX] = q[:, HALO + CX - 1]

    shape = (EXT_Y, NZ)
    ends = {
        0: (iota(shape, 0) == 0, iota(shape, 0) == EXT_Y - 1),
        1: (iota(shape, 1) == 0, iota(shape, 1) == NZ - 1),
    }

    def primitives(q, x):
        inverse = 1.0 / q[0, x]
        for d in range(3):
            prim[d, x] = q[1 + d, x] * inverse
        prim[3, x] = jnp.sqrt(GAMMA_ADIABATIC * (q[4, x] * inverse))

    def flux(values, speed, d, c, pressure):
        product = values * speed
        return product + pressure if c == 1 + d else product

    def x_faces(q, x):
        u, un = prim[0, x], prim[0, x + 1]
        rate = jnp.maximum(jnp.abs(u) + prim[3, x], jnp.abs(un) + prim[3, x + 1])
        faces = []
        for c in range(6):
            v, vn = q[c, x], q[c, x + 1]
            f = flux(v, u, 0, c, q[4, x])
            fn = flux(vn, un, 0, c, q[4, x + 1])
            faces.append(f + fn - rate * (vn - v))
        return faces

    def update(q, combine, start, stop):
        def fill(x, carry):
            primitives(q, x)
            return carry

        lax.fori_loop(start - 1, stop + 1, fill, 0)
        for c, value in enumerate(x_faces(q, start - 1)):
            face[c] = value

        def row(x, carry):
            upper = x_faces(q, x)
            change = []
            for c in range(6):
                change.append(upper[c] - face[c])
                face[c] = upper[c]
            for axis in (0, 1):
                d = 1 + axis
                size = shape[axis]
                lower_end, upper_end = ends[axis]
                u = prim[d, x]
                a = jnp.abs(u) + prim[3, x]
                un = pltpu.roll(u, size - 1, axis)
                rate = jnp.maximum(a, pltpu.roll(a, size - 1, axis))
                p = q[4, x]
                pn = pltpu.roll(p, size - 1, axis)
                for c in range(6):
                    v = q[c, x]
                    vn = pn if c == 4 else pltpu.roll(v, size - 1, axis)
                    f = flux(v, u, d, c, p)
                    g = f + flux(vn, un, d, c, pn) - rate * (vn - v)
                    twice = f + f
                    g = jnp.where(upper_end, twice, g)
                    below = jnp.where(lower_end, twice, pltpu.roll(g, 1, axis))
                    change[c] = change[c] + (g - below)
            for c in range(6):
                combine(c, x, q[c, x] - (0.5 * LAM) * change[c])
            return carry

        lax.fori_loop(start, stop, row, 0)

    ghosts(q0)

    def first_section(c, x, value):
        q1[c, x] = value

    update(q0, first_section, 1, EXT_X - 1)
    ghosts(q1)

    def second_section(c, x, value):
        q2[c, x] = 0.75 * q0[c, x] + 0.25 * value

    update(q1, second_section, 2, EXT_X - 2)
    ghosts(q2)

    def third_section(c, x, value):
        q1[c, x] = q0[c, x] * (1.0 / 3.0) + (2.0 / 3.0) * value

    update(q2, third_section, HALO, HALO + CX)
    out_ref[...] = q1[:, inner, own, :]


def whole(shape):
    return pl.BlockSpec(shape, lambda *_: (0,) * len(shape))


def call(kernel, outs, scratch=(), **more):
    return pl.pallas_call(
        kernel,
        out_shape=outs,
        scratch_shapes=list(scratch),
        compiler_params=compiler_params(),
        **more,
    )


def deliver(buffer):
    return lax.all_to_all(buffer, AXES, split_axis=0, concat_axis=0, tiled=True)


def integrate_parcels(owner, rank, live, answered, parcels, steps=4):
    size = BLK_DEV // steps
    block = pl.BlockSpec((5, size, LANES), lambda s: (0, s, 0))
    small = whole((CHUNKS, LANES))
    return pl.pallas_call(
        parcel_kernel,
        grid=(steps,),
        in_specs=[small, small, small, whole((DEVICES, LANES)), block],
        out_specs=[block, whole((DEVICES, LANES))],
        out_shape=[
            jax.ShapeDtypeStruct((5, BLK_DEV, LANES), F32),
            jax.ShapeDtypeStruct((DEVICES, LANES), F32),
        ],
        scratch_shapes=[
            pltpu.VMEM((LANES, LANES), BF16),
            pltpu.VMEM((LANES, PIECES * LANES), BF16),
            pltpu.VMEM((PIECES * LANES, NVAR * LANES), BF16),
            pltpu.VMEM((NVAR * LANES, LANES), BF16),
        ],
        compiler_params=compiler_params(),
    )(owner, rank, live, answered, parcels)


def body(gas_state, particle_blocks, owner, host_cell, live_count):
    gas, pair = lax.axis_index("gas"), lax.axis_index("grp")
    count = lax.axis_size("gas")
    owner = owner.reshape(CHUNKS, LANES)
    host_cell = host_cell.reshape(CHUNKS, LANES)
    live = live_count.reshape(CHUNKS, LANES)
    square = jax.ShapeDtypeStruct((DEVICES, LANES), F32)

    requests, rank = call(
        request_kernel,
        [
            jax.ShapeDtypeStruct((DEVICES, LANES), jnp.int32),
            jax.ShapeDtypeStruct((CHUNKS, LANES), jnp.int32),
        ],
    )(owner, host_cell)
    asked = deliver(requests)

    edge = lax.dynamic_slice_in_dim(gas_state, (1 - pair) * (CY - 8), 8, axis=2)
    edge = lax.ppermute(edge, "grp", [(0, 1), (1, 0)])
    upward = jnp.concatenate([gas_state[:, CX - HALO :], edge[:, CX - HALO :]], axis=2)
    downward = jnp.concatenate([gas_state[:, :HALO], edge[:, :HALO]], axis=2)
    low = lax.ppermute(upward, "gas", [(i, (i + 1) % count) for i in range(count)])
    high = lax.ppermute(downward, "gas", [((i + 1) % count, i) for i in range(count)])

    flat = gas_state.reshape(6, ROWS, NZ)
    table = call(
        table_kernel,
        jax.ShapeDtypeStruct((NVAR * LANES, PIECES * 2 * ROWS), BF16),
    )(flat)
    replies = call(gather_kernel, square, [pltpu.VMEM((LANES, LANES), F32)])(asked, table)
    answered = deliver(replies)

    parcels_next, sources = integrate_parcels(owner, rank, live, answered, particle_blocks)
    come = deliver(sources)

    place = jnp.stack([pair, gas == 0, gas == count - 1]).astype(jnp.int32)
    extended = pltpu.VMEM((6, EXT_X, EXT_Y, NZ), F32)
    vmem = pl.BlockSpec(memory_space=pltpu.VMEM)
    section_three = call(
        gas_kernel,
        jax.ShapeDtypeStruct((6, CX, CY, NZ), F32),
        [
            extended,
            extended,
            extended,
            pltpu.VMEM((4, EXT_X, EXT_Y, NZ), F32),
            pltpu.VMEM((6, EXT_Y, NZ), F32),
        ],
        in_specs=[pl.BlockSpec(memory_space=pltpu.SMEM)] + [vmem] * 4,
    )(place, gas_state, edge, low, high)

    gas_next = call(
        scatter_kernel,
        jax.ShapeDtypeStruct((6, ROWS, NZ), F32),
        [pltpu.VMEM((NVAR * LANES, 2 * ROWS), F32)],
    )(asked, come, section_three.reshape(6, ROWS, NZ))
    return (gas_next.reshape(6, CX, CY, NZ), parcels_next)


def solution(mesh):
    placed = (
        P(None, "gas", "grp", None),
        P(None, AXES, None),
        P(AXES, None),
        P(AXES),
        P(AXES),
    )
    return jax.shard_map(
        body,
        mesh=mesh,
        in_specs=placed,
        out_specs=(P(None, "gas", "grp", None), P(None, AXES, None)),
        check_vma=False,
    )
```

```python
import jax
import jax.numpy as jnp
from jax import lax
from jax.experimental import pallas as pl
from jax.experimental.pallas import tpu as pltpu
from jax.sharding import PartitionSpec as P

AXES = ("gas", "grp")
DEVICES = 128
LANES = 128
CAP = 16
CX, CY, NZ = 4, 32, 256
ROWS = CX * CY
BLK_DEV = 1024
CHUNKS = BLK_DEV // LANES
NSUB = 4
NVAR = 5
PIECES = 3
HALO = 3
PART = 256
PARCEL_FLOPS = 10**10
EXT_X = CX + 2 * HALO
EXT_Y = CY + 8

LAM = 0.1
GAMMA_ADIABATIC = 1.4
CLOCK_INCREMENT = 0.25
TAU_DRAG = 0.8
THERMAL_RELAX = 1.2
EVAP_RATE = 0.5
LATENT_EVAPORATE = 0.3
WEIGHT = 0.05
LOG2E = 1.4426950408889634

F32 = jnp.float32
BF16 = jnp.bfloat16
MIB = 1024 * 1024


def iota(shape, dim):
    return lax.broadcasted_iota(jnp.int32, shape, dim)


def dot(a, b):
    return lax.dot_general(a, b, (((1,), (0,)), ((), ())), preferred_element_type=F32)


def dot_nt(a, b):
    return lax.dot_general(a, b, (((1,), (1,)), ((), ())), preferred_element_type=F32)


def split(x):
    pieces = []
    for _ in range(PIECES):
        piece = x.astype(BF16)
        pieces.append(piece)
        x = x - piece.astype(F32)
    return pieces


def ones_where(mask):
    return jnp.where(mask, 1.0, 0.0).astype(BF16)


def compiler_params(mib):
    return pltpu.CompilerParams(vmem_limit_bytes=mib * MIB)


def request_kernel(owner_ref, cell_ref, req_ref, rank_ref):
    down = iota((LANES, LANES), 0)
    across = iota((LANES, 2 * LANES), 1)
    earlier = ones_where((iota((LANES, 2 * LANES), 0) < across) | (across >= LANES))
    named = [down == owner_ref[i : i + 1, :] for i in range(CHUNKS)]
    hots = [ones_where(n) for n in named]
    counts = dot(jnp.concatenate(hots, axis=0), earlier)
    before = jnp.zeros((LANES, LANES), F32)
    slots = iota((CAP, LANES), 0)
    highs, lows = [], []
    for i in range(CHUNKS):
        count = counts[i * LANES : (i + 1) * LANES]
        place = jnp.where(named[i], count[:, :LANES] + before, 0.0)
        rank = jnp.sum(place, axis=0, keepdims=True).astype(jnp.int32)
        rank_ref[i : i + 1, :] = rank
        before = before + count[:, LANES:]
        cell = cell_ref[i : i + 1, :]
        placed = slots == rank
        highs.append(jnp.where(placed, (((cell >> 8) + 1) << 8).astype(F32), 0.0))
        lows.append(jnp.where(placed, (cell & 255).astype(F32), 0.0))
    values = jnp.concatenate(highs + lows, axis=1).astype(BF16)
    total = dot_nt(jnp.concatenate(hots + hots, axis=1), values)
    req_ref[...] = jnp.full((DEVICES, LANES), -1, jnp.int32)
    req_ref[:, :CAP] = total.astype(jnp.int32) - 256


def outward_kernel(gas_ref, edge_ref, table_ref, up_ref, down_ref):
    inverse = 1.0 / gas_ref[0].reshape(ROWS, NZ)
    for c in range(NVAR):
        value = gas_ref[1 + c].reshape(ROWS, NZ) * inverse
        for half in range(2):
            turned = value[:, half * LANES : (half + 1) * LANES].T
            for p, piece in enumerate(split(turned)):
                start = p * 2 * ROWS + half * ROWS
                table_ref[c * LANES : (c + 1) * LANES, start : start + ROWS] = piece
    for i in range(HALO):
        here = slice(i * CY, (i + 1) * CY)
        up_ref[:, here, :] = gas_ref[:, CX - HALO + i]
        down_ref[:, here, :] = gas_ref[:, i]
    at = HALO * CY

    def corners(near, after):
        for ref, one, two in ((up_ref, CX - 1, CX - 2), (down_ref, 0, 1)):
            ref[:, at : at + 8, :] = jnp.zeros((6, 8, NZ), F32)
            ref[:, at : at + 1, :] = edge_ref[:, one, near : near + 1, :]
            ref[:, at + 1 : at + 2, :] = edge_ref[:, one, after : after + 1, :]
            ref[:, at + 2 : at + 3, :] = edge_ref[:, two, near : near + 1, :]

    pair = lax.axis_index("grp")
    pl.when(pair == 0)(lambda: corners(0, 1))
    pl.when(pair == 1)(lambda: corners(7, 6))


def cell_parts(asked_ref):
    cell = asked_ref[...].astype(F32).T.astype(jnp.int32)
    return (cell >> 8) + ROWS * ((cell >> 7) & 1), cell & (LANES - 1)


def gather_kernel(asked_ref, table_ref, reply_ref, found):
    row, lane = cell_parts(asked_ref)
    table = table_ref[...]
    found[...] = jnp.zeros((LANES, LANES), F32)
    for pair in range(CAP // 2):
        k = 2 * pair
        rows = jnp.concatenate([row[k : k + 1], row[k + 1 : k + 2]], axis=1)
        lanes = jnp.concatenate([lane[k : k + 1], lane[k + 1 : k + 2]], axis=1)
        hot = ones_where(iota((2 * ROWS, 2 * LANES), 0) == rows)
        values = dot(table, jnp.concatenate([hot] * PIECES, axis=0))
        here = iota((LANES, 2 * LANES), 0) == lanes
        for c in range(NVAR):
            part = values[c * LANES : (c + 1) * LANES]
            picked = jnp.sum(jnp.where(here, part, 0.0), axis=0, keepdims=True)
            found[c * CAP + k : c * CAP + k + 1, :] = picked[:, :LANES]
            found[c * CAP + k + 1 : c * CAP + k + 2, :] = picked[:, LANES:]
    reply_ref[...] = found[...].T


def integrate(parcels, gas_vars):
    mass, speeds, thermal = parcels[0], parcels[1:4], parcels[4]
    ambient, vapor = gas_vars[3], gas_vars[4]
    power = first_power = (-2.0 / 3.0) * jnp.log2(mass)
    exposure = None
    rate = CLOCK_INCREMENT * EVAP_RATE * LOG2E
    headroom = rate * (0.3 - vapor)
    offset = ambient + LATENT_EVAPORATE
    for _ in range(NSUB):
        inverse = jnp.exp2(power)
        square = 1.0 + thermal * thermal
        guess = pl.reciprocal(square, approx=True)
        guess = guess * (2.0 - square * guess)
        loss = (headroom - (0.3 * rate) * guess) * inverse
        kept = jnp.exp2((-CLOCK_INCREMENT / THERMAL_RELAX * LOG2E) * inverse)
        thermal = offset + (thermal - ambient) * kept - LATENT_EVAPORATE * jnp.exp2(loss)
        power = power + (2.0 / 3.0) * loss
        exposure = inverse if exposure is None else exposure + inverse
    drag = jnp.exp2((-CLOCK_INCREMENT / TAU_DRAG * LOG2E) * exposure)
    moved = [gas_vars[c] + (speeds[c] - gas_vars[c]) * drag for c in range(3)]
    return [mass * jnp.exp2(1.5 * (first_power - power))] + moved + [thermal]


def parcel_kernel(
    owner_ref, rank_ref, live_ref, ans_ref, old_ref, new_ref, send_ref,
    held, made, hot, turned, slots, alive, spread, placed, answered, got, sent, arrived,
):
    parts = BLK_DEV // PART
    asking = pltpu.make_async_copy(ans_ref, answered, arrived)
    asking.start()
    fetches = []
    for part in range(parts):
        here = slice(part * PART, (part + 1) * PART)
        fetches.append(pltpu.make_async_copy(old_ref.at[:, here, :], held.at[:, here, :], got.at[part]))
        fetches[part].start()

    pad = jnp.zeros((LANES - 3 * CHUNKS, LANES), F32)
    rows = [owner_ref[...], rank_ref[...], live_ref[...]]
    stack = jnp.concatenate([r.astype(F32) for r in rows] + [pad], axis=0)
    columns = stack.T.astype(BF16)
    across = iota((LANES, LANES), 1)
    down = iota((LANES, LANES), 0)
    for i in range(CHUNKS):
        shape = (LANES, 3 * LANES)
        chosen = ones_where(iota(shape, 0) == i + CHUNKS * (iota(shape, 1) // LANES))
        wide = dot(columns, chosen).astype(jnp.int32)
        owner, rank, live = (wide[:, s * LANES : (s + 1) * LANES] for s in range(3))
        here = slice(i * LANES, (i + 1) * LANES)
        hot[here, :] = ones_where(owner == across)
        slots[here, :] = ones_where(across % CAP == rank)
        alive[here, :] = jnp.where(across < live, 1.0, 0.0)
        turned[:, here] = ones_where(down == owner_ref[i : i + 1, :])
    shape = (PIECES * LANES, NVAR * LANES)
    spread[...] = ones_where((iota(shape, 0) % LANES) // CAP == iota(shape, 1) // LANES)

    asking.wait()
    answers = jnp.concatenate(split(answered[...]), axis=1)
    kind = iota((PART, LANES), 1) // CAP
    stores = []
    for part in range(parts):
        here = slice(part * PART, (part + 1) * PART)
        slot = slots[here, :]
        received = dot(hot[here, :], answers).astype(BF16)
        wide = dot(received * jnp.concatenate([slot] * PIECES, axis=1), spread[...])
        gas_vars = [wide[:, c * LANES : (c + 1) * LANES] for c in range(NVAR)]
        fetches[part].wait()
        old = [held[c, here, :] for c in range(5)]
        living = alive[here, :] > 0.0
        new = [jnp.where(living, n, o) for n, o in zip(integrate(old, gas_vars), old)]
        for c in range(5):
            made[c, here, :] = new[c]
        stores.append(pltpu.make_async_copy(made.at[:, here, :], new_ref.at[:, here, :], sent.at[part]))
        stores[part].start()
        change = [old[0] - new[0]] + [old[0] * old[c] - new[0] * new[c] for c in range(1, 5)]
        total = jnp.zeros((PART, LANES), F32)
        for c in range(NVAR):
            total = jnp.where(kind == c, jnp.sum(change[c], axis=1, keepdims=True), total)
        for p, piece in enumerate(split(total)):
            placed[here, p * LANES : (p + 1) * LANES] = piece * slot
    send = dot(turned[...], placed[...])
    send_ref[...] = sum(send[:, p * LANES : (p + 1) * LANES] for p in range(PIECES))
    for store in stores:
        store.wait()


def scatter_kernel(asked_ref, come_ref, section_ref, out_ref, total):
    row, lane = cell_parts(asked_ref)
    pieces = [p.astype(F32) for p in split(come_ref[...].T)]
    for pair in range(CAP // 2):
        hots, parts = [], []
        for k in (2 * pair, 2 * pair + 1):
            hot = ones_where(iota((2 * ROWS, LANES), 0) == row[k : k + 1])
            here = iota((LANES, LANES), 0) == lane[k : k + 1]
            for piece in pieces:
                hots.append(hot)
                parts.append(
                    jnp.concatenate(
                        [
                            jnp.where(here, piece[c * CAP + k : c * CAP + k + 1], 0.0)
                            for c in range(NVAR)
                        ],
                        axis=0,
                    ).astype(BF16)
                )
        added = dot_nt(jnp.concatenate(parts, axis=1), jnp.concatenate(hots, axis=1))
        if pair == 0:
            total[...] = added
        else:
            total[...] += added
    for c in range(NVAR):
        for half in range(2):
            cells = WEIGHT * total[c * LANES : (c + 1) * LANES, half * ROWS : (half + 1) * ROWS].T
            z = slice(half * LANES, (half + 1) * LANES)
            out_ref[c, :, z] = section_ref[c, :, z] + cells
            if c == 0:
                out_ref[NVAR, :, z] = section_ref[NVAR, :, z] + cells


def gas_kernel(gas_ref, edge_ref, low_ref, high_ref, out_ref, q0, q1, q2, prim, face):
    place, pair = lax.axis_index("gas"), lax.axis_index("grp")
    own = pl.ds(pl.multiple_of(pair * 8, 8), CY)
    side = pl.ds(pl.multiple_of((1 - pair) * CY, 8), 8)
    inner = slice(HALO, HALO + CX)
    q0[:, inner, own, :] = gas_ref[...]
    q0[:, inner, side, :] = edge_ref[...]
    for i in range(HALO):
        q0[:, i, own, :] = low_ref[:, i * CY : (i + 1) * CY, :]
        q0[:, HALO + CX + i, own, :] = high_ref[:, i * CY : (i + 1) * CY, :]

    def corners(near, after):
        at = HALO * CY
        for ref, one, two in ((low_ref, HALO - 1, HALO - 2), (high_ref, HALO + CX, HALO + CX + 1)):
            q0[:, one, near : near + 1, :] = ref[:, at : at + 1, :]
            q0[:, one, after : after + 1, :] = ref[:, at + 1 : at + 2, :]
            q0[:, two, near : near + 1, :] = ref[:, at + 2 : at + 3, :]

    pl.when(pair == 0)(lambda: corners(CY, CY + 1))
    pl.when(pair == 1)(lambda: corners(7, 6))

    def ghosts(q):
        @pl.when(place == 0)
        def _():
            q[:, HALO - 1] = q[:, HALO]

        @pl.when(place == lax.axis_size("gas") - 1)
        def _():
            q[:, HALO + CX] = q[:, HALO + CX - 1]

    row_in_tile = iota((8, NZ), 0)
    lane = iota((EXT_Y, LANES), 1)

    def above(v, axis):
        if axis == 0:
            moved = pltpu.roll(v, EXT_Y - 1, 0)
            tail = jnp.where(row_in_tile == 7, v[EXT_Y - 8 :], moved[EXT_Y - 8 :])
            return jnp.concatenate([moved[: EXT_Y - 8], tail], axis=0)
        left, right = v[:, :LANES], v[:, LANES:]
        left_moved, right_moved = pltpu.roll(left, LANES - 1, 1), pltpu.roll(right, LANES - 1, 1)
        at_end = lane == LANES - 1
        return jnp.concatenate(
            [jnp.where(at_end, right_moved, left_moved), jnp.where(at_end, right, right_moved)], axis=1
        )

    def below(g, first, axis):
        if axis == 0:
            moved = pltpu.roll(g, 1, 0)
            head = jnp.where(row_in_tile == 0, first, moved[:8])
            return jnp.concatenate([head, moved[8:]], axis=0)
        left, right = pltpu.roll(g[:, :LANES], 1, 1), pltpu.roll(g[:, LANES:], 1, 1)
        at_start = lane == 0
        return jnp.concatenate(
            [jnp.where(at_start, first, left), jnp.where(at_start, left, right)], axis=1
        )

    def primitives(q, x):
        inverse = 1.0 / q[0, x]
        for d in range(3):
            prim[d, x] = q[1 + d, x] * inverse
        prim[3, x] = jnp.sqrt(GAMMA_ADIABATIC * (q[4, x] * inverse))

    def x_faces(q, x):
        u, un = prim[0, x], prim[0, x + 1]
        rate = jnp.maximum(jnp.abs(u) + prim[3, x], jnp.abs(un) + prim[3, x + 1])
        here, there = u + rate, un - rate
        faces = []
        for c in range(6):
            g = q[c, x] * here + q[c, x + 1] * there
            faces.append(g + (q[4, x] + q[4, x + 1]) if c == 1 else g)
        return faces

    def update(q, combine, start, stop):
        def fill(x, carry):
            primitives(q, x)
            return carry

        lax.fori_loop(start - 1, stop + 1, fill, 0)
        for c, value in enumerate(x_faces(q, start - 1)):
            face[c] = value

        def row(x, carry):
            change = []
            for c, upper in enumerate(x_faces(q, x)):
                change.append(upper - face[c])
                face[c] = upper
            for axis in (0, 1):
                d = 1 + axis
                start_cells = (slice(0, 8), slice(None)) if axis == 0 else (slice(None), slice(0, LANES))
                u = prim[d, x]
                a = jnp.abs(u) + prim[3, x]
                un = above(u, axis)
                rate = jnp.maximum(a, above(a, axis))
                here, there = u + rate, un - rate
                for c in range(6):
                    v = q[c, x]
                    g = v * here + above(v, axis) * there
                    first = 2.0 * (v[start_cells] * u[start_cells])
                    if c == 1 + d:
                        p = q[4, x]
                        g = g + (p + above(p, axis))
                        first = first + 2.0 * p[start_cells]
                    change[c] = change[c] + (g - below(g, first, axis))
            for c in range(6):
                combine(c, x, q[c, x] - (0.5 * LAM) * change[c])
            return carry

        lax.fori_loop(start, stop, row, 0)

    ghosts(q0)

    def first_section(c, x, value):
        q1[c, x] = value

    update(q0, first_section, 1, EXT_X - 1)
    ghosts(q1)

    def second_section(c, x, value):
        q2[c, x] = 0.75 * q0[c, x] + 0.25 * value

    update(q1, second_section, 2, EXT_X - 2)
    ghosts(q2)

    def third_section(c, x, value):
        q1[c, x] = q0[c, x] * (1.0 / 3.0) + (2.0 / 3.0) * value

    update(q2, third_section, HALO, HALO + CX)
    out_ref[...] = q1[:, inner, own, :]


SMALL = pl.CostEstimate(flops=1, bytes_accessed=1, transcendentals=0)


def call(kernel, mib, outs, scratch=(), cost=SMALL, **more):
    return pl.pallas_call(
        kernel,
        out_shape=outs,
        scratch_shapes=list(scratch),
        compiler_params=compiler_params(mib),
        cost_estimate=cost,
        **more,
    )


def deliver(buffer):
    return lax.all_to_all(buffer, AXES, split_axis=0, concat_axis=0, tiled=True)


def integrate_parcels(owner, rank, live, answered, parcels):
    held = pl.BlockSpec(memory_space=pltpu.VMEM)
    far = pl.BlockSpec(memory_space=pl.ANY)
    return call(
        parcel_kernel,
        60,
        [
            jax.ShapeDtypeStruct((5, BLK_DEV, LANES), F32),
            jax.ShapeDtypeStruct((DEVICES, LANES), F32),
        ],
        [
            pltpu.VMEM((5, BLK_DEV, LANES), F32),
            pltpu.VMEM((5, BLK_DEV, LANES), F32),
            pltpu.VMEM((BLK_DEV, DEVICES), BF16),
            pltpu.VMEM((DEVICES, BLK_DEV), BF16),
            pltpu.VMEM((BLK_DEV, LANES), BF16),
            pltpu.VMEM((BLK_DEV, LANES), F32),
            pltpu.VMEM((PIECES * LANES, NVAR * LANES), BF16),
            pltpu.VMEM((BLK_DEV, PIECES * LANES), BF16),
            pltpu.VMEM((DEVICES, LANES), F32),
            pltpu.SemaphoreType.DMA((BLK_DEV // PART,)),
            pltpu.SemaphoreType.DMA((BLK_DEV // PART,)),
            pltpu.SemaphoreType.DMA,
        ],
        cost=pl.CostEstimate(flops=PARCEL_FLOPS, bytes_accessed=8 * 5 * BLK_DEV * LANES, transcendentals=0),
        in_specs=[held, held, held, far, far],
        out_specs=[far, held],
    )(owner, rank, live, answered, parcels)


def body(gas_state, particle_blocks, owner, host_cell, live_count):
    pair = lax.axis_index("grp")
    count = lax.axis_size("gas")
    owner = owner.reshape(CHUNKS, LANES)
    host_cell = host_cell.reshape(CHUNKS, LANES)
    live = live_count.reshape(CHUNKS, LANES)
    square = jax.ShapeDtypeStruct((DEVICES, LANES), F32)

    requests, rank = call(
        request_kernel,
        60,
        [
            jax.ShapeDtypeStruct((DEVICES, LANES), jnp.int32),
            jax.ShapeDtypeStruct((CHUNKS, LANES), jnp.int32),
        ],
    )(owner, host_cell)
    asked = deliver(requests)

    mine, _ = lax.optimization_barrier((gas_state, requests))
    edge = lax.dynamic_slice_in_dim(mine, (1 - pair) * (CY - 8), 8, axis=2)
    edge = lax.ppermute(edge, "grp", [(0, 1), (1, 0)])
    message = jax.ShapeDtypeStruct((6, HALO * CY + 8, NZ), F32)
    table, upward, downward = call(
        outward_kernel,
        12,
        [jax.ShapeDtypeStruct((NVAR * LANES, PIECES * 2 * ROWS), BF16), message, message],
    )(gas_state, edge)
    replies = call(gather_kernel, 16, square, [pltpu.VMEM((LANES, LANES), F32)])(asked, table)
    answered = deliver(replies)

    upward, downward, _ = lax.optimization_barrier((upward, downward, replies))
    low = lax.ppermute(upward, "gas", [(i, (i + 1) % count) for i in range(count)])
    high = lax.ppermute(downward, "gas", [((i + 1) % count, i) for i in range(count)])
    parcels_next, sources = integrate_parcels(owner, rank, live, answered, particle_blocks)
    come = deliver(sources)

    low, high, _ = lax.optimization_barrier((low, high, sources))
    extended = pltpu.VMEM((6, EXT_X, EXT_Y, NZ), F32)
    section_three = call(
        gas_kernel,
        28,
        jax.ShapeDtypeStruct((6, CX, CY, NZ), F32),
        [
            extended,
            extended,
            extended,
            pltpu.VMEM((4, EXT_X, EXT_Y, NZ), F32),
            pltpu.VMEM((6, EXT_Y, NZ), F32),
        ],
    )(gas_state, edge, low, high)

    gas_next = call(
        scatter_kernel,
        20,
        jax.ShapeDtypeStruct((6, ROWS, NZ), F32),
        [pltpu.VMEM((NVAR * LANES, 2 * ROWS), F32)],
    )(asked, come, section_three.reshape(6, ROWS, NZ))
    return (gas_next.reshape(6, CX, CY, NZ), parcels_next)


def solution(mesh):
    placed = (
        P(None, "gas", "grp", None),
        P(None, AXES, None),
        P(AXES, None),
        P(AXES),
        P(AXES),
    )
    return jax.shard_map(
        body,
        mesh=mesh,
        in_specs=placed,
        out_specs=(P(None, "gas", "grp", None), P(None, AXES, None)),
        check_vma=False,
    )
```

```python
import jax
import jax.numpy as jnp
from jax import lax
from jax.experimental import pallas as pl
from jax.experimental.pallas import tpu as pltpu
from jax.sharding import PartitionSpec as P

AXES = ("gas", "grp")
DEVICES = 128
LANES = 128
CAP = 16
CX, CY, NZ = 4, 32, 256
ROWS = CX * CY
BLK_DEV = 1024
CHUNKS = BLK_DEV // LANES
NSUB = 4
NVAR = 5
PIECES = 2
HALO = 3
PART = 256
PARCEL_FLOPS = 10**10
EXT_X = CX + 2 * HALO
EXT_Y = CY + 8

LAM = 0.1
GAMMA_ADIABATIC = 1.4
CLOCK_INCREMENT = 0.25
TAU_DRAG = 0.8
THERMAL_RELAX = 1.2
EVAP_RATE = 0.5
LATENT_EVAPORATE = 0.3
WEIGHT = 0.05
LOG2E = 1.4426950408889634

F32 = jnp.float32
BF16 = jnp.bfloat16
MIB = 1024 * 1024


def iota(shape, dim):
    return lax.broadcasted_iota(jnp.int32, shape, dim)


def dot(a, b):
    return lax.dot_general(a, b, (((1,), (0,)), ((), ())), preferred_element_type=F32)


def dot_nt(a, b):
    return lax.dot_general(a, b, (((1,), (1,)), ((), ())), preferred_element_type=F32)


def split(x):
    pieces = []
    for _ in range(PIECES):
        piece = x.astype(BF16)
        pieces.append(piece)
        x = x - piece.astype(F32)
    return pieces


def ones_where(mask):
    return jnp.where(mask, 1.0, 0.0).astype(BF16)


def compiler_params(mib):
    return pltpu.CompilerParams(vmem_limit_bytes=mib * MIB)


def request_kernel(owner_ref, cell_ref, req_ref, rank_ref):
    down = iota((LANES, LANES), 0)
    across = iota((LANES, 2 * LANES), 1)
    earlier = ones_where((iota((LANES, 2 * LANES), 0) < across) | (across >= LANES))
    named = [down == owner_ref[i : i + 1, :] for i in range(CHUNKS)]
    hots = [ones_where(n) for n in named]
    counts = dot(jnp.concatenate(hots, axis=0), earlier)
    before = jnp.zeros((LANES, LANES), F32)
    slots = iota((CAP, LANES), 0)
    highs, lows = [], []
    for i in range(CHUNKS):
        count = counts[i * LANES : (i + 1) * LANES]
        place = jnp.where(named[i], count[:, :LANES] + before, 0.0)
        rank = jnp.sum(place, axis=0, keepdims=True).astype(jnp.int32)
        rank_ref[i : i + 1, :] = rank
        before = before + count[:, LANES:]
        cell = cell_ref[i : i + 1, :]
        placed = slots == rank
        highs.append(jnp.where(placed, (((cell >> 8) + 1) << 8).astype(F32), 0.0))
        lows.append(jnp.where(placed, (cell & 255).astype(F32), 0.0))
    values = jnp.concatenate(highs + lows, axis=1).astype(BF16)
    total = dot_nt(jnp.concatenate(hots + hots, axis=1), values)
    req_ref[...] = jnp.full((DEVICES, LANES), -1, jnp.int32)
    req_ref[:, :CAP] = total.astype(jnp.int32) - 256


def table_kernel(gas_ref, table_ref):
    inverse = 1.0 / gas_ref[0].reshape(ROWS, NZ)
    for c in range(NVAR):
        value = gas_ref[1 + c].reshape(ROWS, NZ) * inverse
        for half in range(2):
            turned = value[:, half * LANES : (half + 1) * LANES].T
            for p, piece in enumerate(split(turned)):
                start = p * 2 * ROWS + half * ROWS
                table_ref[c * LANES : (c + 1) * LANES, start : start + ROWS] = piece


def message_kernel(gas_ref, edge_ref, up_ref, down_ref):
    for i in range(HALO):
        here = slice(i * CY, (i + 1) * CY)
        up_ref[:, here, :] = gas_ref[:, CX - HALO + i]
        down_ref[:, here, :] = gas_ref[:, i]
    at = HALO * CY

    def corners(near, after):
        for ref, one, two in ((up_ref, CX - 1, CX - 2), (down_ref, 0, 1)):
            ref[:, at : at + 8, :] = jnp.zeros((6, 8, NZ), F32)
            ref[:, at : at + 1, :] = edge_ref[:, one, near : near + 1, :]
            ref[:, at + 1 : at + 2, :] = edge_ref[:, one, after : after + 1, :]
            ref[:, at + 2 : at + 3, :] = edge_ref[:, two, near : near + 1, :]

    pair = lax.axis_index("grp")
    pl.when(pair == 0)(lambda: corners(0, 1))
    pl.when(pair == 1)(lambda: corners(7, 6))


def cell_parts(asked_ref):
    cell = asked_ref[...].astype(F32).T.astype(jnp.int32)
    return (cell >> 8) + ROWS * ((cell >> 7) & 1), cell & (LANES - 1)


def gather_kernel(asked_ref, table_ref, reply_ref, found):
    row, lane = cell_parts(asked_ref)
    table = table_ref[...]
    found[...] = jnp.zeros((LANES, LANES), F32)
    for pair in range(CAP // 2):
        k = 2 * pair
        rows = jnp.concatenate([row[k : k + 1], row[k + 1 : k + 2]], axis=1)
        lanes = jnp.concatenate([lane[k : k + 1], lane[k + 1 : k + 2]], axis=1)
        hot = ones_where(iota((2 * ROWS, 2 * LANES), 0) == rows)
        values = dot(table, jnp.concatenate([hot] * PIECES, axis=0))
        here = iota((LANES, 2 * LANES), 0) == lanes
        for c in range(NVAR):
            part = values[c * LANES : (c + 1) * LANES]
            picked = jnp.sum(jnp.where(here, part, 0.0), axis=0, keepdims=True)
            found[c * CAP + k : c * CAP + k + 1, :] = picked[:, :LANES]
            found[c * CAP + k + 1 : c * CAP + k + 2, :] = picked[:, LANES:]
    reply_ref[...] = found[...].T


def integrate(parcels, gas_vars):
    mass, speeds, thermal = parcels[0], parcels[1:4], parcels[4]
    ambient, vapor = gas_vars[3], gas_vars[4]
    power = first_power = (-2.0 / 3.0) * jnp.log2(mass)
    exposure = None
    rate = CLOCK_INCREMENT * EVAP_RATE * LOG2E
    headroom = rate * (0.3 - vapor)
    offset = ambient + LATENT_EVAPORATE
    for _ in range(NSUB):
        inverse = jnp.exp2(power)
        square = 1.0 + thermal * thermal
        guess = pl.reciprocal(square, approx=True)
        guess = guess * (2.0 - square * guess)
        loss = (headroom - (0.3 * rate) * guess) * inverse
        kept = jnp.exp2((-CLOCK_INCREMENT / THERMAL_RELAX * LOG2E) * inverse)
        thermal = offset + (thermal - ambient) * kept - LATENT_EVAPORATE * jnp.exp2(loss)
        power = power + (2.0 / 3.0) * loss
        exposure = inverse if exposure is None else exposure + inverse
    drag = jnp.exp2((-CLOCK_INCREMENT / TAU_DRAG * LOG2E) * exposure)
    moved = [gas_vars[c] + (speeds[c] - gas_vars[c]) * drag for c in range(3)]
    return [mass * jnp.exp2(1.5 * (first_power - power))] + moved + [thermal]


def parcel_kernel(
    owner_ref, rank_ref, live_ref, ans_ref, old_ref, new_ref, send_ref,
    held, made, hot, turned, slots, alive, spread, placed, outgoing, got, sent, posted,
):
    parts = BLK_DEV // PART
    fetches = []
    for part in range(parts):
        here = slice(part * PART, (part + 1) * PART)
        fetches.append(pltpu.make_async_copy(old_ref.at[:, here, :], held.at[:, here, :], got.at[part]))
        fetches[part].start()

    pad = jnp.zeros((LANES - 3 * CHUNKS, LANES), F32)
    rows = [owner_ref[...], rank_ref[...], live_ref[...]]
    stack = jnp.concatenate([r.astype(F32) for r in rows] + [pad], axis=0)
    columns = stack.T.astype(BF16)
    across = iota((LANES, LANES), 1)
    down = iota((LANES, LANES), 0)
    for i in range(CHUNKS):
        shape = (LANES, 3 * LANES)
        chosen = ones_where(iota(shape, 0) == i + CHUNKS * (iota(shape, 1) // LANES))
        wide = dot(columns, chosen).astype(jnp.int32)
        owner, rank, live = (wide[:, s * LANES : (s + 1) * LANES] for s in range(3))
        here = slice(i * LANES, (i + 1) * LANES)
        hot[here, :] = ones_where(owner == across)
        slots[here, :] = ones_where(across % CAP == rank)
        alive[here, :] = jnp.where(across < live, 1.0, 0.0)
        turned[:, here] = ones_where(down == owner_ref[i : i + 1, :])
    shape = (PIECES * LANES, NVAR * LANES)
    spread[...] = ones_where((iota(shape, 0) % LANES) // CAP == iota(shape, 1) // LANES)

    answers = jnp.concatenate(split(ans_ref[...]), axis=1)
    kind = iota((PART, LANES), 1) // CAP
    stores = []
    for part in range(parts):
        here = slice(part * PART, (part + 1) * PART)
        slot = slots[here, :]
        received = dot(hot[here, :], answers).astype(BF16)
        wide = dot(received * jnp.concatenate([slot] * PIECES, axis=1), spread[...])
        gas_vars = [wide[:, c * LANES : (c + 1) * LANES] for c in range(NVAR)]
        fetches[part].wait()
        old = [held[c, here, :] for c in range(5)]
        living = alive[here, :] > 0.0
        new = [jnp.where(living, n, o) for n, o in zip(integrate(old, gas_vars), old)]
        for c in range(5):
            made[c, here, :] = new[c]
        stores.append(pltpu.make_async_copy(made.at[:, here, :], new_ref.at[:, here, :], sent.at[part]))
        stores[part].start()
        change = [old[0] - new[0]] + [old[0] * old[c] - new[0] * new[c] for c in range(1, 5)]
        total = jnp.zeros((PART, LANES), F32)
        for c in range(NVAR):
            total = jnp.where(kind == c, jnp.sum(change[c], axis=1, keepdims=True), total)
        for p, piece in enumerate(split(total)):
            placed[here, p * LANES : (p + 1) * LANES] = piece * slot
    send = dot(turned[...], placed[...])
    outgoing[...] = sum(send[:, p * LANES : (p + 1) * LANES] for p in range(PIECES))
    post = pltpu.make_async_copy(outgoing, send_ref, posted)
    post.start()
    for store in stores:
        store.wait()
    post.wait()


def scatter_kernel(asked_ref, come_ref, section_ref, out_ref, total, made, sent):
    row, lane = cell_parts(asked_ref)
    pieces = [p.astype(F32) for p in split(come_ref[...].T)]
    for pair in range(CAP // 2):
        hots, parts = [], []
        for k in (2 * pair, 2 * pair + 1):
            hot = ones_where(iota((2 * ROWS, LANES), 0) == row[k : k + 1])
            here = iota((LANES, LANES), 0) == lane[k : k + 1]
            for piece in pieces:
                hots.append(hot)
                parts.append(
                    jnp.concatenate(
                        [
                            jnp.where(here, piece[c * CAP + k : c * CAP + k + 1], 0.0)
                            for c in range(NVAR)
                        ],
                        axis=0,
                    ).astype(BF16)
                )
        added = dot_nt(jnp.concatenate(parts, axis=1), jnp.concatenate(hots, axis=1))
        if pair == 0:
            total[...] = added
        else:
            total[...] += added
    copies = []

    def send(c):
        copies.append(pltpu.make_async_copy(made.at[c], out_ref.at[c], sent.at[c]))
        copies[-1].start()

    for c in range(NVAR):
        for half in range(2):
            cells = WEIGHT * total[c * LANES : (c + 1) * LANES, half * ROWS : (half + 1) * ROWS].T
            z = slice(half * LANES, (half + 1) * LANES)
            made[c, :, z] = section_ref[c, :, z] + cells
            if c == 0:
                made[NVAR, :, z] = section_ref[NVAR, :, z] + cells
        send(c)
        if c == 0:
            send(NVAR)
    for copy in copies:
        copy.wait()


def gas_kernel(gas_ref, edge_ref, low_ref, high_ref, out_ref, q0, q1, q2, prim, face):
    place, pair = lax.axis_index("gas"), lax.axis_index("grp")
    own = pl.ds(pl.multiple_of(pair * 8, 8), CY)
    side = pl.ds(pl.multiple_of((1 - pair) * CY, 8), 8)
    inner = slice(HALO, HALO + CX)
    q0[:, inner, own, :] = gas_ref[...]
    q0[:, inner, side, :] = edge_ref[...]
    for i in range(HALO):
        q0[:, i, own, :] = low_ref[:, i * CY : (i + 1) * CY, :]
        q0[:, HALO + CX + i, own, :] = high_ref[:, i * CY : (i + 1) * CY, :]

    def corners(near, after):
        at = HALO * CY
        for ref, one, two in ((low_ref, HALO - 1, HALO - 2), (high_ref, HALO + CX, HALO + CX + 1)):
            q0[:, one, near : near + 1, :] = ref[:, at : at + 1, :]
            q0[:, one, after : after + 1, :] = ref[:, at + 1 : at + 2, :]
            q0[:, two, near : near + 1, :] = ref[:, at + 2 : at + 3, :]

    pl.when(pair == 0)(lambda: corners(CY, CY + 1))
    pl.when(pair == 1)(lambda: corners(7, 6))

    def ghosts(q):
        @pl.when(place == 0)
        def _():
            q[:, HALO - 1] = q[:, HALO]

        @pl.when(place == lax.axis_size("gas") - 1)
        def _():
            q[:, HALO + CX] = q[:, HALO + CX - 1]

    tiles, halves = EXT_Y // 8, range(NZ // LANES)
    row_in_tile, lane = iota((8, LANES), 0), iota((8, LANES), 1)

    def at(ref, c, x, t):
        return [ref[c, x, 8 * t : 8 * t + 8, h * LANES : (h + 1) * LANES] for h in halves]

    def each(f, *lists):
        return [f(*items) for items in zip(*lists)]

    def y_turned(v):
        return [pltpu.roll(part, 7, 0) for part in v]

    def y_above(v, turned, turned_next):
        after = v if turned_next is None else turned_next
        return each(lambda m, n: jnp.where(row_in_tile == 7, n, m), turned, after)

    def z_above(v):
        left, right = (pltpu.roll(part, LANES - 1, 1) for part in v)
        return [jnp.where(lane == LANES - 1, right, left), jnp.where(lane == LANES - 1, v[1], right)]

    def z_below(g, first):
        left, right = (pltpu.roll(part, 1, 1) for part in g)
        return [jnp.where(lane == 0, first, left), jnp.where(lane == 0, left, right)]

    def weights(u, sound, un, soundn):
        rate = each(lambda u, s, un, sn: jnp.maximum(jnp.abs(u) + s, jnp.abs(un) + sn), u, sound, un, soundn)
        return each(jnp.add, u, rate), each(jnp.subtract, un, rate)

    def face_flux(v, here, vn, there, p=None, pn=None):
        g = each(lambda v, w, vn, wn: v * w + vn * wn, v, here, vn, there)
        return g if p is None else each(lambda g, p, pn: g + (p + pn), g, p, pn)

    def primitives(q, x):
        inverse = 1.0 / q[0, x]
        for d in range(3):
            prim[d, x] = q[1 + d, x] * inverse
        prim[3, x] = jnp.sqrt(GAMMA_ADIABATIC * (q[4, x] * inverse))

    def x_faces(q, x, t):
        here, there = weights(at(prim, 0, x, t), at(prim, 3, x, t), at(prim, 0, x + 1, t), at(prim, 3, x + 1, t))
        faces = []
        for c in range(6):
            pressure = (at(q, 4, x, t), at(q, 4, x + 1, t)) if c == 1 else ()
            faces.append(face_flux(at(q, c, x, t), here, at(q, c, x + 1, t), there, *pressure))
        return faces

    def update(q, combine, start, stop):
        def fill(x, carry):
            primitives(q, x)
            return carry

        lax.fori_loop(start - 1, stop + 1, fill, 0)
        for t in range(tiles):
            for c, value in enumerate(x_faces(q, start - 1, t)):
                for h in halves:
                    face[c, 8 * t : 8 * t + 8, h * LANES : (h + 1) * LANES] = value[h]

        def row(x, carry):
            turned = [y_turned(at(q, c, x, 0)) for c in range(6)]
            turned_u, turned_s = y_turned(at(prim, 1, x, 0)), y_turned(at(prim, 3, x, 0))
            shifted = [None] * 6
            for t in range(tiles):
                rows = slice(8 * t, 8 * t + 8)
                final = t == tiles - 1
                v = [at(q, c, x, t) for c in range(6)]
                sound = at(prim, 3, x, t)

                change = []
                for c, upper in enumerate(x_faces(q, x, t)):
                    z = [slice(h * LANES, (h + 1) * LANES) for h in halves]
                    change.append([upper[h] - face[c, rows, z[h]] for h in halves])
                    for h in halves:
                        face[c, rows, z[h]] = upper[h]

                u = at(prim, 1, x, t)
                next_u = None if final else y_turned(at(prim, 1, x, t + 1))
                next_s = None if final else y_turned(at(prim, 3, x, t + 1))
                here, there = weights(u, sound, y_above(u, turned_u, next_u), y_above(sound, turned_s, next_s))
                turned_u, turned_s = next_u, next_s
                next_v = [None if final else y_turned(at(q, c, x, t + 1)) for c in range(6)]
                above = [y_above(v[c], turned[c], next_v[c]) for c in range(6)]
                turned = next_v
                for c in range(6):
                    pressure = (v[4], above[4]) if c == 2 else ()
                    g = face_flux(v[c], here, above[c], there, *pressure)
                    moved = [pltpu.roll(part, 1, 0) for part in g]
                    if t == 0:
                        first = each(lambda v, u: 2.0 * (v * u), v[c], u)
                        if c == 2:
                            first = each(lambda f, p: f + 2.0 * p, first, v[4])
                    else:
                        first = shifted[c]
                    below = each(lambda f, m: jnp.where(row_in_tile == 0, f, m), first, moved)
                    shifted[c] = moved
                    change[c] = each(lambda k, g, b: k + (g - b), change[c], g, below)

                u = at(prim, 2, x, t)
                here, there = weights(u, sound, z_above(u), z_above(sound))
                above_p = z_above(v[4])
                for c in range(6):
                    above_v = above_p if c == 4 else z_above(v[c])
                    pressure = (v[4], above_p) if c == 3 else ()
                    g = face_flux(v[c], here, above_v, there, *pressure)
                    first = 2.0 * (v[c][0] * u[0])
                    if c == 3:
                        first = first + 2.0 * v[4][0]
                    below = z_below(g, first)
                    change[c] = each(lambda k, g, b: k + (g - b), change[c], g, below)

                for c in range(6):
                    for h in halves:
                        z = slice(h * LANES, (h + 1) * LANES)
                        combine(c, x, rows, z, v[c][h] - (0.5 * LAM) * change[c][h])
            return carry

        lax.fori_loop(start, stop, row, 0)

    ghosts(q0)

    def first_section(c, x, rows, z, value):
        q1[c, x, rows, z] = value

    update(q0, first_section, 1, EXT_X - 1)
    ghosts(q1)

    def second_section(c, x, rows, z, value):
        q2[c, x, rows, z] = 0.75 * q0[c, x, rows, z] + 0.25 * value

    update(q1, second_section, 2, EXT_X - 2)
    ghosts(q2)

    def third_section(c, x, rows, z, value):
        q1[c, x, rows, z] = q0[c, x, rows, z] * (1.0 / 3.0) + (2.0 / 3.0) * value

    update(q2, third_section, HALO, HALO + CX)
    out_ref[...] = q1[:, inner, own, :]


LARGE_FLOPS = 10**9
LARGE = pl.CostEstimate(flops=LARGE_FLOPS, bytes_accessed=1, transcendentals=0)
SMALL = pl.CostEstimate(flops=1, bytes_accessed=1, transcendentals=0)


def call(kernel, mib, outs, scratch=(), cost=SMALL, **more):
    return pl.pallas_call(
        kernel,
        out_shape=outs,
        scratch_shapes=list(scratch),
        compiler_params=compiler_params(mib),
        cost_estimate=cost,
        **more,
    )


def deliver(buffer):
    return lax.all_to_all(buffer, AXES, split_axis=0, concat_axis=0, tiled=True)


HELD = pl.BlockSpec(memory_space=pltpu.VMEM)
ANYWHERE = pl.BlockSpec(memory_space=pl.ANY)


def in_hbm(array):
    return pltpu.with_memory_space_constraint(array, pltpu.HBM)


def integrate_parcels(owner, rank, live, answered, parcels):
    return call(
        parcel_kernel,
        24,
        [
            jax.ShapeDtypeStruct((5, BLK_DEV, LANES), F32),
            jax.ShapeDtypeStruct((DEVICES, LANES), F32),
        ],
        [
            pltpu.VMEM((5, BLK_DEV, LANES), F32),
            pltpu.VMEM((5, BLK_DEV, LANES), F32),
            pltpu.VMEM((BLK_DEV, DEVICES), BF16),
            pltpu.VMEM((DEVICES, BLK_DEV), BF16),
            pltpu.VMEM((BLK_DEV, LANES), BF16),
            pltpu.VMEM((BLK_DEV, LANES), F32),
            pltpu.VMEM((PIECES * LANES, NVAR * LANES), BF16),
            pltpu.VMEM((BLK_DEV, PIECES * LANES), BF16),
            pltpu.VMEM((DEVICES, LANES), F32),
            pltpu.SemaphoreType.DMA((BLK_DEV // PART,)),
            pltpu.SemaphoreType.DMA((BLK_DEV // PART,)),
            pltpu.SemaphoreType.DMA,
        ],
        cost=pl.CostEstimate(flops=PARCEL_FLOPS, bytes_accessed=8 * 5 * BLK_DEV * LANES, transcendentals=0),
        in_specs=[HELD] * 4 + [ANYWHERE],
        out_specs=[ANYWHERE, ANYWHERE],
    )(owner, rank, live, answered, in_hbm(parcels))


def body(gas_state, particle_blocks, owner, host_cell, live_count):
    pair = lax.axis_index("grp")
    count = lax.axis_size("gas")
    owner = owner.reshape(CHUNKS, LANES)
    host_cell = host_cell.reshape(CHUNKS, LANES)
    live = live_count.reshape(CHUNKS, LANES)
    square = jax.ShapeDtypeStruct((DEVICES, LANES), F32)

    requests, rank = call(
        request_kernel,
        8,
        [
            jax.ShapeDtypeStruct((DEVICES, LANES), jnp.int32),
            jax.ShapeDtypeStruct((CHUNKS, LANES), jnp.int32),
        ],
    )(in_hbm(owner), in_hbm(host_cell))
    asked = deliver(requests)

    mine, _ = lax.optimization_barrier((gas_state, requests))
    edge = lax.dynamic_slice_in_dim(mine, (1 - pair) * (CY - 8), 8, axis=2)
    edge = lax.ppermute(edge, "grp", [(0, 1), (1, 0)])
    table = call(
        table_kernel, 12, jax.ShapeDtypeStruct((NVAR * LANES, PIECES * 2 * ROWS), BF16)
    )(mine)
    replies = call(gather_kernel, 16, square, [pltpu.VMEM((LANES, LANES), F32)], cost=LARGE)(asked, table)
    answered = deliver(replies)

    edge, replies = lax.optimization_barrier((edge, replies))
    message = jax.ShapeDtypeStruct((6, HALO * CY + 8, NZ), F32)
    upward, downward = call(message_kernel, 12, [message, message])(gas_state, edge)
    low = lax.ppermute(upward, "gas", [(i, (i + 1) % count) for i in range(count)])
    high = lax.ppermute(downward, "gas", [((i + 1) % count, i) for i in range(count)])
    parcels_next, sources = integrate_parcels(owner, rank, live, answered, particle_blocks)
    come = deliver(sources)

    low, high, _ = lax.optimization_barrier((low, high, sources))
    extended = pltpu.VMEM((6, EXT_X, EXT_Y, NZ), F32)
    section_three = call(
        gas_kernel,
        28,
        jax.ShapeDtypeStruct((6, CX, CY, NZ), F32),
        [
            extended,
            extended,
            extended,
            pltpu.VMEM((4, EXT_X, EXT_Y, NZ), F32),
            pltpu.VMEM((6, EXT_Y, NZ), F32),
        ],
    )(gas_state, edge, low, high)

    gas_next = call(
        scatter_kernel,
        20,
        jax.ShapeDtypeStruct((6, ROWS, NZ), F32),
        [
            pltpu.VMEM((NVAR * LANES, 2 * ROWS), F32),
            pltpu.VMEM((6, ROWS, NZ), F32),
            pltpu.SemaphoreType.DMA((6,)),
        ],
        out_specs=ANYWHERE,
    )(asked, come, section_three.reshape(6, ROWS, NZ))
    return (gas_next.reshape(6, CX, CY, NZ), parcels_next)


def solution(mesh):
    placed = (
        P(None, "gas", "grp", None),
        P(None, AXES, None),
        P(AXES, None),
        P(AXES),
        P(AXES),
    )
    return jax.shard_map(
        body,
        mesh=mesh,
        in_specs=placed,
        out_specs=(P(None, "gas", "grp", None), P(None, AXES, None)),
        check_vma=False,
    )
```

```python
import jax
import jax.numpy as jnp
from jax import lax
from jax.experimental import pallas as pl
from jax.experimental.pallas import tpu as pltpu
from jax.sharding import PartitionSpec as P

AXES = ("gas", "grp")
DEVICES = 128
LANES = 128
CAP = 16
CX, CY, NZ = 4, 32, 256
ROWS = CX * CY
BLK_DEV = 1024
CHUNKS = BLK_DEV // LANES
NSUB = 4
NVAR = 5
PIECES = 2
HALO = 3
FAR = HALO - 1
PART = 256
PARCEL_FLOPS = 10**10
EXT_X = CX + 2 * HALO
EXT_Y = CY + 8

LAM = 0.1
GAMMA_ADIABATIC = 1.4
CLOCK_INCREMENT = 0.25
TAU_DRAG = 0.8
THERMAL_RELAX = 1.2
EVAP_RATE = 0.5
LATENT_EVAPORATE = 0.3
WEIGHT = 0.05
LOG2E = 1.4426950408889634

F32 = jnp.float32
BF16 = jnp.bfloat16
MIB = 1024 * 1024


def iota(shape, dim):
    return lax.broadcasted_iota(jnp.int32, shape, dim)


def dot(a, b):
    return lax.dot_general(a, b, (((1,), (0,)), ((), ())), preferred_element_type=F32)


def dot_nt(a, b):
    return lax.dot_general(a, b, (((1,), (1,)), ((), ())), preferred_element_type=F32)


def split(x):
    pieces = []
    for _ in range(PIECES):
        piece = x.astype(BF16)
        pieces.append(piece)
        x = x - piece.astype(F32)
    return pieces


def ones_where(mask):
    return jnp.where(mask, 1.0, 0.0).astype(BF16)


def compiler_params(mib):
    return pltpu.CompilerParams(vmem_limit_bytes=mib * MIB)


def request_kernel(owner_ref, cell_ref, req_ref, rank_ref):
    down = iota((LANES, LANES), 0)
    across = iota((LANES, 2 * LANES), 1)
    earlier = ones_where((iota((LANES, 2 * LANES), 0) < across) | (across >= LANES))
    named = [down == owner_ref[i : i + 1, :] for i in range(CHUNKS)]
    hots = [ones_where(n) for n in named]
    counts = dot(jnp.concatenate(hots, axis=0), earlier)
    before = jnp.zeros((LANES, LANES), F32)
    slots = iota((CAP, LANES), 0)
    highs, lows = [], []
    for i in range(CHUNKS):
        count = counts[i * LANES : (i + 1) * LANES]
        place = jnp.where(named[i], count[:, :LANES] + before, 0.0)
        rank = jnp.sum(place, axis=0, keepdims=True).astype(jnp.int32)
        rank_ref[i : i + 1, :] = rank
        before = before + count[:, LANES:]
        cell = cell_ref[i : i + 1, :]
        placed = slots == rank
        highs.append(jnp.where(placed, (((cell >> 8) + 1) << 8).astype(F32), 0.0))
        lows.append(jnp.where(placed, (cell & 255).astype(F32), 0.0))
    values = jnp.concatenate(highs + lows, axis=1).astype(BF16)
    total = dot_nt(jnp.concatenate(hots + hots, axis=1), values)
    req_ref[...] = jnp.full((DEVICES, LANES), -1, jnp.int32)
    req_ref[:, :CAP] = total.astype(jnp.int32) - 256


def by_core(action, *refs):
    pair = lax.axis_index("grp")
    for core in range(2):
        pl.when(pair == core)(lambda: action(core, *refs))


def table_kernel(gas_ref, table_ref, first_ref, second_ref):
    def outermost(pair, up_ref, down_ref):
        up_ref[...] = gas_ref[:, CX - 1]
        down_ref[...] = gas_ref[:, 0]

    by_core(outermost, first_ref, second_ref)
    inverse = 1.0 / gas_ref[0].reshape(ROWS, NZ)
    for c in range(NVAR):
        value = gas_ref[1 + c].reshape(ROWS, NZ) * inverse
        for half in range(2):
            turned = value[:, half * LANES : (half + 1) * LANES].T
            for p, piece in enumerate(split(turned)):
                start = p * 2 * ROWS + half * ROWS
                table_ref[c * LANES : (c + 1) * LANES, start : start + ROWS] = piece


def message_kernel(gas_ref, edge_ref, first_ref, second_ref):
    at = FAR * CY

    def fill(pair, up_ref, down_ref):
        near, after = ((0, 1), (7, 6))[pair]
        for i in range(FAR):
            here = slice(i * CY, (i + 1) * CY)
            up_ref[:, here, :] = gas_ref[:, CX - HALO + i]
            down_ref[:, here, :] = gas_ref[:, 1 + i]
        for ref, one, two in ((up_ref, CX - 1, CX - 2), (down_ref, 0, 1)):
            ref[:, at : at + 8, :] = jnp.zeros((6, 8, NZ), F32)
            ref[:, at : at + 1, :] = edge_ref[:, one, near : near + 1, :]
            ref[:, at + 1 : at + 2, :] = edge_ref[:, one, after : after + 1, :]
            ref[:, at + 2 : at + 3, :] = edge_ref[:, two, near : near + 1, :]

    by_core(fill, first_ref, second_ref)


def cell_parts(asked_ref):
    cell = asked_ref[...].astype(F32).T.astype(jnp.int32)
    return (cell >> 8) + ROWS * ((cell >> 7) & 1), cell & (LANES - 1)


def gather_kernel(asked_ref, table_ref, reply_ref, found):
    row, lane = cell_parts(asked_ref)
    table = table_ref[...]
    found[...] = jnp.zeros((LANES, LANES), F32)
    for pair in range(CAP // 2):
        k = 2 * pair
        rows = jnp.concatenate([row[k : k + 1], row[k + 1 : k + 2]], axis=1)
        lanes = jnp.concatenate([lane[k : k + 1], lane[k + 1 : k + 2]], axis=1)
        hot = ones_where(iota((2 * ROWS, 2 * LANES), 0) == rows)
        values = dot(table, jnp.concatenate([hot] * PIECES, axis=0))
        here = iota((LANES, 2 * LANES), 0) == lanes
        for c in range(NVAR):
            part = values[c * LANES : (c + 1) * LANES]
            picked = jnp.sum(jnp.where(here, part, 0.0), axis=0, keepdims=True)
            found[c * CAP + k : c * CAP + k + 1, :] = picked[:, :LANES]
            found[c * CAP + k + 1 : c * CAP + k + 2, :] = picked[:, LANES:]
    reply_ref[...] = found[...].T


def integrate(parcels, gas_vars):
    mass, speeds, thermal = parcels[0], parcels[1:4], parcels[4]
    ambient, vapor = gas_vars[3], gas_vars[4]
    power = first_power = (-2.0 / 3.0) * jnp.log2(mass)
    exposure = None
    rate = CLOCK_INCREMENT * EVAP_RATE * LOG2E
    headroom = rate * (0.3 - vapor)
    offset = ambient + LATENT_EVAPORATE
    for _ in range(NSUB):
        inverse = jnp.exp2(power)
        square = 1.0 + thermal * thermal
        guess = pl.reciprocal(square, approx=True)
        guess = guess * (2.0 - square * guess)
        loss = (headroom - (0.3 * rate) * guess) * inverse
        kept = jnp.exp2((-CLOCK_INCREMENT / THERMAL_RELAX * LOG2E) * inverse)
        thermal = offset + (thermal - ambient) * kept - LATENT_EVAPORATE * jnp.exp2(loss)
        power = power + (2.0 / 3.0) * loss
        exposure = inverse if exposure is None else exposure + inverse
    drag = jnp.exp2((-CLOCK_INCREMENT / TAU_DRAG * LOG2E) * exposure)
    moved = [gas_vars[c] + (speeds[c] - gas_vars[c]) * drag for c in range(3)]
    return [mass * jnp.exp2(1.5 * (first_power - power))] + moved + [thermal]


def parcel_kernel(
    owner_ref, rank_ref, live_ref, ans_ref, old_ref, new_ref, send_ref,
    held, made, hot, turned, slots, alive, spread, placed, outgoing, got, sent, posted,
):
    parts = BLK_DEV // PART
    fetches = []
    for part in range(parts):
        here = slice(part * PART, (part + 1) * PART)
        fetches.append(pltpu.make_async_copy(old_ref.at[:, here, :], held.at[:, here, :], got.at[part]))
        fetches[part].start()

    pad = jnp.zeros((LANES - 3 * CHUNKS, LANES), F32)
    rows = [owner_ref[...], rank_ref[...], live_ref[...]]
    stack = jnp.concatenate([r.astype(F32) for r in rows] + [pad], axis=0)
    columns = stack.T.astype(BF16)
    across = iota((LANES, LANES), 1)
    down = iota((LANES, LANES), 0)
    for i in range(CHUNKS):
        shape = (LANES, 3 * LANES)
        chosen = ones_where(iota(shape, 0) == i + CHUNKS * (iota(shape, 1) // LANES))
        wide = dot(columns, chosen).astype(jnp.int32)
        owner, rank, live = (wide[:, s * LANES : (s + 1) * LANES] for s in range(3))
        here = slice(i * LANES, (i + 1) * LANES)
        hot[here, :] = ones_where(owner == across)
        slots[here, :] = ones_where(across % CAP == rank)
        alive[here, :] = jnp.where(across < live, 1.0, 0.0)
        turned[:, here] = ones_where(down == owner_ref[i : i + 1, :])
    shape = (PIECES * LANES, NVAR * LANES)
    spread[...] = ones_where((iota(shape, 0) % LANES) // CAP == iota(shape, 1) // LANES)

    answers = jnp.concatenate(split(ans_ref[...]), axis=1)
    kind = iota((PART, LANES), 1) // CAP
    stores = []
    for part in range(parts):
        here = slice(part * PART, (part + 1) * PART)
        slot = slots[here, :]
        received = dot(hot[here, :], answers).astype(BF16)
        wide = dot(received * jnp.concatenate([slot] * PIECES, axis=1), spread[...])
        gas_vars = [wide[:, c * LANES : (c + 1) * LANES] for c in range(NVAR)]
        fetches[part].wait()
        old = [held[c, here, :] for c in range(5)]
        living = alive[here, :] > 0.0
        new = [jnp.where(living, n, o) for n, o in zip(integrate(old, gas_vars), old)]
        for c in range(5):
            made[c, here, :] = new[c]
        stores.append(pltpu.make_async_copy(made.at[:, here, :], new_ref.at[:, here, :], sent.at[part]))
        stores[part].start()
        change = [old[0] - new[0]] + [old[0] * old[c] - new[0] * new[c] for c in range(1, 5)]
        total = jnp.zeros((PART, LANES), F32)
        for c in range(NVAR):
            total = jnp.where(kind == c, jnp.sum(change[c], axis=1, keepdims=True), total)
        for p, piece in enumerate(split(total)):
            placed[here, p * LANES : (p + 1) * LANES] = piece * slot
    send = dot(turned[...], placed[...])
    outgoing[...] = sum(send[:, p * LANES : (p + 1) * LANES] for p in range(PIECES))
    post = pltpu.make_async_copy(outgoing, send_ref, posted)
    post.start()
    for store in stores:
        store.wait()
    post.wait()


def scatter_kernel(asked_ref, come_ref, section_ref, out_ref, total, made, sent):
    row, lane = cell_parts(asked_ref)
    pieces = [p.astype(F32) for p in split(come_ref[...].T)]
    for pair in range(CAP // 2):
        hots, parts = [], []
        for k in (2 * pair, 2 * pair + 1):
            hot = ones_where(iota((2 * ROWS, LANES), 0) == row[k : k + 1])
            here = iota((LANES, LANES), 0) == lane[k : k + 1]
            for piece in pieces:
                hots.append(hot)
                parts.append(
                    jnp.concatenate(
                        [
                            jnp.where(here, piece[c * CAP + k : c * CAP + k + 1], 0.0)
                            for c in range(NVAR)
                        ],
                        axis=0,
                    ).astype(BF16)
                )
        added = dot_nt(jnp.concatenate(parts, axis=1), jnp.concatenate(hots, axis=1))
        if pair == 0:
            total[...] = added
        else:
            total[...] += added
    copies = []

    def send(c):
        copies.append(pltpu.make_async_copy(made.at[c], out_ref.at[c], sent.at[c]))
        copies[-1].start()

    for c in range(NVAR):
        for half in range(2):
            cells = WEIGHT * total[c * LANES : (c + 1) * LANES, half * ROWS : (half + 1) * ROWS].T
            z = slice(half * LANES, (half + 1) * LANES)
            made[c, :, z] = section_ref[c, :, z] + cells
            if c == 0:
                made[NVAR, :, z] = section_ref[NVAR, :, z] + cells
        send(c)
        if c == 0:
            send(NVAR)
    for copy in copies:
        copy.wait()


def gas_kernel(gas_ref, edge_ref, below, above, low, high, out_ref, q0, q1, q2, prim, face):
    place, pair = lax.axis_index("gas"), lax.axis_index("grp")
    own = pl.ds(pl.multiple_of(pair * 8, 8), CY)
    side = pl.ds(pl.multiple_of((1 - pair) * CY, 8), 8)
    inner = slice(HALO, HALO + CX)
    q0[:, inner, own, :] = gas_ref[...]
    q0[:, inner, side, :] = edge_ref[...]
    at_corner = FAR * CY

    def rows_beside(pair, below_ref, above_ref):
        mine = slice(8 * pair, 8 * pair + CY)
        q0[:, HALO - 1, mine, :] = below_ref[...]
        q0[:, HALO + CX, mine, :] = above_ref[...]

    def rows_beyond(pair, low_ref, high_ref):
        mine = slice(8 * pair, 8 * pair + CY)
        near, after = ((CY, CY + 1), (7, 6))[pair]
        for i in range(FAR):
            q0[:, i, mine, :] = low_ref[:, i * CY : (i + 1) * CY, :]
            q0[:, HALO + CX + 1 + i, mine, :] = high_ref[:, i * CY : (i + 1) * CY, :]
        for ref, one, two in ((low_ref, HALO - 1, HALO - 2), (high_ref, HALO + CX, HALO + CX + 1)):
            q0[:, one, near : near + 1, :] = ref[:, at_corner : at_corner + 1, :]
            q0[:, one, after : after + 1, :] = ref[:, at_corner + 1 : at_corner + 2, :]
            q0[:, two, near : near + 1, :] = ref[:, at_corner + 2 : at_corner + 3, :]

    by_core(rows_beside, below, above)
    by_core(rows_beyond, low, high)

    def ghosts(q):
        @pl.when(place == 0)
        def _():
            q[:, HALO - 1] = q[:, HALO]

        @pl.when(place == lax.axis_size("gas") - 1)
        def _():
            q[:, HALO + CX] = q[:, HALO + CX - 1]

    tiles, halves = EXT_Y // 8, range(NZ // LANES)
    row_in_tile, lane = iota((8, LANES), 0), iota((8, LANES), 1)

    def at(ref, c, x, t):
        return [ref[c, x, 8 * t : 8 * t + 8, h * LANES : (h + 1) * LANES] for h in halves]

    def each(f, *lists):
        return [f(*items) for items in zip(*lists)]

    def y_turned(v):
        return [pltpu.roll(part, 7, 0) for part in v]

    def y_above(v, turned, turned_next):
        after = v if turned_next is None else turned_next
        return each(lambda m, n: jnp.where(row_in_tile == 7, n, m), turned, after)

    def z_above(v):
        left, right = (pltpu.roll(part, LANES - 1, 1) for part in v)
        return [jnp.where(lane == LANES - 1, right, left), jnp.where(lane == LANES - 1, v[1], right)]

    def z_below(g, first):
        left, right = (pltpu.roll(part, 1, 1) for part in g)
        return [jnp.where(lane == 0, first, left), jnp.where(lane == 0, left, right)]

    def weights(u, sound, un, soundn):
        rate = each(lambda u, s, un, sn: jnp.maximum(jnp.abs(u) + s, jnp.abs(un) + sn), u, sound, un, soundn)
        return each(jnp.add, u, rate), each(jnp.subtract, un, rate)

    def face_flux(v, here, vn, there, p=None, pn=None):
        g = each(lambda v, w, vn, wn: v * w + vn * wn, v, here, vn, there)
        return g if p is None else each(lambda g, p, pn: g + (p + pn), g, p, pn)

    def primitives(q, x):
        inverse = 1.0 / q[0, x]
        for d in range(3):
            prim[d, x] = q[1 + d, x] * inverse
        prim[3, x] = jnp.sqrt(GAMMA_ADIABATIC * (q[4, x] * inverse))

    def x_faces(q, x, t):
        here, there = weights(at(prim, 0, x, t), at(prim, 3, x, t), at(prim, 0, x + 1, t), at(prim, 3, x + 1, t))
        faces = []
        for c in range(6):
            pressure = (at(q, 4, x, t), at(q, 4, x + 1, t)) if c == 1 else ()
            faces.append(face_flux(at(q, c, x, t), here, at(q, c, x + 1, t), there, *pressure))
        return faces

    def update(q, combine, start, stop):
        def fill(x, carry):
            primitives(q, x)
            return carry

        lax.fori_loop(start - 1, stop + 1, fill, 0, unroll=2)
        for t in range(tiles):
            for c, value in enumerate(x_faces(q, start - 1, t)):
                for h in halves:
                    face[c, 8 * t : 8 * t + 8, h * LANES : (h + 1) * LANES] = value[h]

        def row(x, carry):
            turned = [y_turned(at(q, c, x, 0)) for c in range(6)]
            turned_u, turned_s = y_turned(at(prim, 1, x, 0)), y_turned(at(prim, 3, x, 0))
            shifted = [None] * 6
            for t in range(tiles):
                rows = slice(8 * t, 8 * t + 8)
                final = t == tiles - 1
                v = [at(q, c, x, t) for c in range(6)]
                sound = at(prim, 3, x, t)

                change = []
                for c, upper in enumerate(x_faces(q, x, t)):
                    z = [slice(h * LANES, (h + 1) * LANES) for h in halves]
                    change.append([upper[h] - face[c, rows, z[h]] for h in halves])
                    for h in halves:
                        face[c, rows, z[h]] = upper[h]

                u = at(prim, 1, x, t)
                next_u = None if final else y_turned(at(prim, 1, x, t + 1))
                next_s = None if final else y_turned(at(prim, 3, x, t + 1))
                here, there = weights(u, sound, y_above(u, turned_u, next_u), y_above(sound, turned_s, next_s))
                turned_u, turned_s = next_u, next_s
                next_v = [None if final else y_turned(at(q, c, x, t + 1)) for c in range(6)]
                above = [y_above(v[c], turned[c], next_v[c]) for c in range(6)]
                turned = next_v
                for c in range(6):
                    pressure = (v[4], above[4]) if c == 2 else ()
                    g = face_flux(v[c], here, above[c], there, *pressure)
                    moved = [pltpu.roll(part, 1, 0) for part in g]
                    if t == 0:
                        first = each(lambda v, u: 2.0 * (v * u), v[c], u)
                        if c == 2:
                            first = each(lambda f, p: f + 2.0 * p, first, v[4])
                    else:
                        first = shifted[c]
                    below = each(lambda f, m: jnp.where(row_in_tile == 0, f, m), first, moved)
                    shifted[c] = moved
                    change[c] = each(lambda k, g, b: k + (g - b), change[c], g, below)

                u = at(prim, 2, x, t)
                here, there = weights(u, sound, z_above(u), z_above(sound))
                above_p = z_above(v[4])
                for c in range(6):
                    above_v = above_p if c == 4 else z_above(v[c])
                    pressure = (v[4], above_p) if c == 3 else ()
                    g = face_flux(v[c], here, above_v, there, *pressure)
                    first = 2.0 * (v[c][0] * u[0])
                    if c == 3:
                        first = first + 2.0 * v[4][0]
                    below = z_below(g, first)
                    change[c] = each(lambda k, g, b: k + (g - b), change[c], g, below)

                for c in range(6):
                    for h in halves:
                        z = slice(h * LANES, (h + 1) * LANES)
                        combine(c, x, rows, z, v[c][h] - (0.5 * LAM) * change[c][h])
            return carry

        lax.fori_loop(start, stop, row, 0)

    ghosts(q0)

    def first_section(c, x, rows, z, value):
        q1[c, x, rows, z] = value

    update(q0, first_section, 1, EXT_X - 1)
    ghosts(q1)

    def second_section(c, x, rows, z, value):
        q2[c, x, rows, z] = 0.75 * q0[c, x, rows, z] + 0.25 * value

    update(q1, second_section, 2, EXT_X - 2)
    ghosts(q2)

    def third_section(c, x, rows, z, value):
        q1[c, x, rows, z] = q0[c, x, rows, z] * (1.0 / 3.0) + (2.0 / 3.0) * value

    update(q2, third_section, HALO, HALO + CX)
    out_ref[...] = q1[:, inner, own, :]


LARGE_FLOPS = 10**9
LARGE = pl.CostEstimate(flops=LARGE_FLOPS, bytes_accessed=1, transcendentals=0)
SMALL = pl.CostEstimate(flops=1, bytes_accessed=1, transcendentals=0)


def call(kernel, mib, outs, scratch=(), cost=SMALL, **more):
    return pl.pallas_call(
        kernel,
        out_shape=outs,
        scratch_shapes=list(scratch),
        compiler_params=compiler_params(mib),
        cost_estimate=cost,
        **more,
    )


def deliver(buffer):
    return lax.all_to_all(buffer, AXES, split_axis=0, concat_axis=0, tiled=True)


HELD = pl.BlockSpec(memory_space=pltpu.VMEM)
ANYWHERE = pl.BlockSpec(memory_space=pl.ANY)


def in_hbm(array):
    return pltpu.with_memory_space_constraint(array, pltpu.HBM)


def integrate_parcels(owner, rank, live, answered, parcels):
    return call(
        parcel_kernel,
        24,
        [
            jax.ShapeDtypeStruct((5, BLK_DEV, LANES), F32),
            jax.ShapeDtypeStruct((DEVICES, LANES), F32),
        ],
        [
            pltpu.VMEM((5, BLK_DEV, LANES), F32),
            pltpu.VMEM((5, BLK_DEV, LANES), F32),
            pltpu.VMEM((BLK_DEV, DEVICES), BF16),
            pltpu.VMEM((DEVICES, BLK_DEV), BF16),
            pltpu.VMEM((BLK_DEV, LANES), BF16),
            pltpu.VMEM((BLK_DEV, LANES), F32),
            pltpu.VMEM((PIECES * LANES, NVAR * LANES), BF16),
            pltpu.VMEM((BLK_DEV, PIECES * LANES), BF16),
            pltpu.VMEM((DEVICES, LANES), F32),
            pltpu.SemaphoreType.DMA((BLK_DEV // PART,)),
            pltpu.SemaphoreType.DMA((BLK_DEV // PART,)),
            pltpu.SemaphoreType.DMA,
        ],
        cost=pl.CostEstimate(flops=PARCEL_FLOPS, bytes_accessed=8 * 5 * BLK_DEV * LANES, transcendentals=0),
        in_specs=[HELD] * 4 + [ANYWHERE],
        out_specs=[ANYWHERE, ANYWHERE],
    )(owner, rank, live, answered, in_hbm(parcels))


def body(gas_state, particle_blocks, owner, host_cell, live_count):
    pair = lax.axis_index("grp")
    count = lax.axis_size("gas")
    owner = owner.reshape(CHUNKS, LANES)
    host_cell = host_cell.reshape(CHUNKS, LANES)
    live = live_count.reshape(CHUNKS, LANES)
    square = jax.ShapeDtypeStruct((DEVICES, LANES), F32)

    requests, rank = call(
        request_kernel,
        8,
        [
            jax.ShapeDtypeStruct((DEVICES, LANES), jnp.int32),
            jax.ShapeDtypeStruct((CHUNKS, LANES), jnp.int32),
        ],
    )(in_hbm(owner), in_hbm(host_cell))
    asked = deliver(requests)

    mine, _ = lax.optimization_barrier((gas_state, requests))
    edge = lax.dynamic_slice_in_dim(mine, (1 - pair) * (CY - 8), 8, axis=2)
    edge = lax.ppermute(edge, "grp", [(0, 1), (1, 0)])
    circuit = [(i, (i + 1) % count) for i in range(count)]
    back = [(target, source) for source, target in circuit]
    row = jax.ShapeDtypeStruct((6, CY, NZ), F32)
    table, first, second = call(
        table_kernel, 12, [jax.ShapeDtypeStruct((NVAR * LANES, PIECES * 2 * ROWS), BF16), row, row]
    )(mine)
    below = lax.ppermute(first, "gas", circuit)
    above = lax.ppermute(second, "gas", back)
    replies = call(gather_kernel, 16, square, [pltpu.VMEM((LANES, LANES), F32)], cost=LARGE)(asked, table)
    answered = deliver(replies)

    edge, below, above, replies = lax.optimization_barrier(
        (edge, below, above, replies)
    )
    message = jax.ShapeDtypeStruct((6, FAR * CY + 8, NZ), F32)
    first, second = call(message_kernel, 12, [message, message])(gas_state, edge)
    low = lax.ppermute(first, "gas", circuit)
    high = lax.ppermute(second, "gas", back)
    parcels_next, sources = integrate_parcels(owner, rank, live, answered, particle_blocks)
    come = deliver(sources)

    below, above, low, high, _ = lax.optimization_barrier(
        (below, above, low, high, sources)
    )
    extended = pltpu.VMEM((6, EXT_X, EXT_Y, NZ), F32)
    section_three = call(
        gas_kernel,
        28,
        jax.ShapeDtypeStruct((6, CX, CY, NZ), F32),
        [
            extended,
            extended,
            extended,
            pltpu.VMEM((4, EXT_X, EXT_Y, NZ), F32),
            pltpu.VMEM((6, EXT_Y, NZ), F32),
        ],
    )(gas_state, edge, below, above, low, high)

    gas_next = call(
        scatter_kernel,
        20,
        jax.ShapeDtypeStruct((6, ROWS, NZ), F32),
        [
            pltpu.VMEM((NVAR * LANES, 2 * ROWS), F32),
            pltpu.VMEM((6, ROWS, NZ), F32),
            pltpu.SemaphoreType.DMA((6,)),
        ],
        out_specs=ANYWHERE,
    )(asked, come, section_three.reshape(6, ROWS, NZ))
    return (gas_next.reshape(6, CX, CY, NZ), parcels_next)


def solution(mesh):
    placed = (
        P(None, "gas", "grp", None),
        P(None, AXES, None),
        P(AXES, None),
        P(AXES),
        P(AXES),
    )
    return jax.shard_map(
        body,
        mesh=mesh,
        in_specs=placed,
        out_specs=(P(None, "gas", "grp", None), P(None, AXES, None)),
        check_vma=False,
    )
```

```python
import jax
import jax.numpy as jnp
from jax import lax
from jax.experimental import pallas as pl
from jax.experimental.pallas import tpu as pltpu
from jax.sharding import PartitionSpec as P

AXES = ("gas", "grp")
DEVICES = 128
LANES = 128
CAP = 16
CX, CY, NZ = 4, 32, 256
ROWS = CX * CY
BLK_DEV = 1024
CHUNKS = BLK_DEV // LANES
NSUB = 4
NVAR = 5
PIECES = 2
HALO = 3
FAR = HALO - 1
PART = 256
GATHERED = 2
SCATTERED = 2
PARCEL_FLOPS = 10**10
EXT_X = CX + 2 * HALO
EXT_Y = CY + 8

LAM = 0.1
GAMMA_ADIABATIC = 1.4
CLOCK_INCREMENT = 0.25
TAU_DRAG = 0.8
THERMAL_RELAX = 1.2
EVAP_RATE = 0.5
LATENT_EVAPORATE = 0.3
WEIGHT = 0.05
LOG2E = 1.4426950408889634

F32 = jnp.float32
BF16 = jnp.bfloat16
MIB = 1024 * 1024


def iota(shape, dim):
    return lax.broadcasted_iota(jnp.int32, shape, dim)


def dot(a, b):
    return lax.dot_general(a, b, (((1,), (0,)), ((), ())), preferred_element_type=F32)


def dot_nt(a, b):
    return lax.dot_general(a, b, (((1,), (1,)), ((), ())), preferred_element_type=F32)


def split(x):
    pieces = []
    for _ in range(PIECES):
        piece = x.astype(BF16)
        pieces.append(piece)
        x = x - piece.astype(F32)
    return pieces


def ones_where(mask):
    return jnp.where(mask, 1.0, 0.0).astype(BF16)


def compiler_params(mib):
    return pltpu.CompilerParams(vmem_limit_bytes=mib * MIB)


def request_kernel(owner_ref, cell_ref, req_ref, rank_ref):
    down = iota((LANES, LANES), 0)
    across = iota((LANES, 2 * LANES), 1)
    earlier = ones_where((iota((LANES, 2 * LANES), 0) < across) | (across >= LANES))
    named = [down == owner_ref[i : i + 1, :] for i in range(CHUNKS)]
    hots = [ones_where(n) for n in named]
    counts = dot(jnp.concatenate(hots, axis=0), earlier)
    before = jnp.zeros((LANES, LANES), F32)
    slots = iota((CAP, LANES), 0)
    highs, lows = [], []
    for i in range(CHUNKS):
        count = counts[i * LANES : (i + 1) * LANES]
        place = jnp.where(named[i], count[:, :LANES] + before, 0.0)
        rank = jnp.sum(place, axis=0, keepdims=True).astype(jnp.int32)
        rank_ref[i : i + 1, :] = rank
        before = before + count[:, LANES:]
        cell = cell_ref[i : i + 1, :]
        placed = slots == rank
        highs.append(jnp.where(placed, (((cell >> 8) + 1) << 8).astype(F32), 0.0))
        lows.append(jnp.where(placed, (cell & 255).astype(F32), 0.0))
    values = jnp.concatenate(highs + lows, axis=1).astype(BF16)
    total = dot_nt(jnp.concatenate(hots + hots, axis=1), values)
    req_ref[...] = jnp.full((DEVICES, LANES), -1, jnp.int32)
    req_ref[:, :CAP] = total.astype(jnp.int32) - 256


def by_core(action, *refs):
    pair = lax.axis_index("grp")
    for core in range(2):
        pl.when(pair == core)(lambda: action(core, *refs))


def table_kernel(gas_ref, table_ref, up_ref, down_ref, edge_ref):
    up_ref[...] = gas_ref[:, CX - 1]
    down_ref[...] = gas_ref[:, 0]

    def beside(pair):
        start = (1 - pair) * (CY - 8)
        edge_ref[...] = gas_ref[:, :, start : start + 8]

    by_core(beside)
    inverse = 1.0 / gas_ref[0].reshape(ROWS, NZ)
    for c in range(NVAR):
        value = gas_ref[1 + c].reshape(ROWS, NZ) * inverse
        for half in range(2):
            turned = value[:, half * LANES : (half + 1) * LANES].T
            for p, piece in enumerate(split(turned)):
                start = p * 2 * ROWS + half * ROWS
                table_ref[c * LANES : (c + 1) * LANES, start : start + ROWS] = piece


def message_kernel(gas_ref, edge_ref, first_ref, second_ref):
    at = FAR * CY

    def fill(pair, up_ref, down_ref):
        near, after = ((0, 1), (7, 6))[pair]
        for i in range(FAR):
            here = slice(i * CY, (i + 1) * CY)
            up_ref[:, here, :] = gas_ref[:, CX - HALO + i]
            down_ref[:, here, :] = gas_ref[:, 1 + i]
        for ref, one, two in ((up_ref, CX - 1, CX - 2), (down_ref, 0, 1)):
            ref[:, at : at + 8, :] = jnp.zeros((6, 8, NZ), F32)
            ref[:, at : at + 1, :] = edge_ref[:, one, near : near + 1, :]
            ref[:, at + 1 : at + 2, :] = edge_ref[:, one, after : after + 1, :]
            ref[:, at + 2 : at + 3, :] = edge_ref[:, two, near : near + 1, :]

    by_core(fill, first_ref, second_ref)


def cell_parts(asked_ref):
    cell = asked_ref[...].astype(F32).T.astype(jnp.int32)
    return (cell >> 8) + ROWS * ((cell >> 7) & 1), cell & (LANES - 1)


def gather_kernel(asked_ref, table_ref, reply_ref, found):
    row, lane = cell_parts(asked_ref)
    table = table_ref[...]
    found[...] = jnp.zeros((LANES, LANES), F32)
    for k in range(0, CAP, GATHERED):
        rows = jnp.concatenate([row[k + j : k + j + 1] for j in range(GATHERED)], axis=1)
        lanes = jnp.concatenate([lane[k + j : k + j + 1] for j in range(GATHERED)], axis=1)
        hot = ones_where(iota((2 * ROWS, GATHERED * LANES), 0) == rows)
        values = dot(table, jnp.concatenate([hot] * PIECES, axis=0))
        here = iota((LANES, GATHERED * LANES), 0) == lanes
        for c in range(NVAR):
            part = values[c * LANES : (c + 1) * LANES]
            picked = jnp.sum(jnp.where(here, part, 0.0), axis=0, keepdims=True)
            for j in range(GATHERED):
                at = c * CAP + k + j
                found[at : at + 1, :] = picked[:, j * LANES : (j + 1) * LANES]
    reply_ref[...] = found[...].T


def integrate(parcels, gas_vars):
    mass, speeds, thermal = parcels[0], parcels[1:4], parcels[4]
    ambient, vapor = gas_vars[3], gas_vars[4]
    power = first_power = (-2.0 / 3.0) * jnp.log2(mass)
    exposure = None
    rate = CLOCK_INCREMENT * EVAP_RATE * LOG2E
    headroom = rate * (0.3 - vapor)
    offset = ambient + LATENT_EVAPORATE
    for _ in range(NSUB):
        inverse = jnp.exp2(power)
        square = 1.0 + thermal * thermal
        guess = pl.reciprocal(square, approx=True)
        guess = guess * (2.0 - square * guess)
        loss = (headroom - (0.3 * rate) * guess) * inverse
        kept = jnp.exp2((-CLOCK_INCREMENT / THERMAL_RELAX * LOG2E) * inverse)
        thermal = offset + (thermal - ambient) * kept - LATENT_EVAPORATE * jnp.exp2(loss)
        power = power + (2.0 / 3.0) * loss
        exposure = inverse if exposure is None else exposure + inverse
    drag = jnp.exp2((-CLOCK_INCREMENT / TAU_DRAG * LOG2E) * exposure)
    moved = [gas_vars[c] + (speeds[c] - gas_vars[c]) * drag for c in range(3)]
    return [mass * jnp.exp2(1.5 * (first_power - power))] + moved + [thermal]


def parcel_kernel(
    owner_ref, rank_ref, live_ref, ans_ref, old_ref, new_ref, send_ref,
    held, made, hot, turned, slots, alive, spread, placed, outgoing, gas_wide, got, sent, posted,
):
    parts = BLK_DEV // PART
    fetches = []
    for part in range(parts):
        here = slice(part * PART, (part + 1) * PART)
        fetches.append(pltpu.make_async_copy(old_ref.at[:, here, :], held.at[:, here, :], got.at[part]))
        fetches[part].start()

    pad = jnp.zeros((LANES - 3 * CHUNKS, LANES), F32)
    rows = [owner_ref[...], rank_ref[...], live_ref[...]]
    stack = jnp.concatenate([r.astype(F32) for r in rows] + [pad], axis=0)
    columns = stack.T.astype(BF16)
    across = iota((LANES, LANES), 1)
    down = iota((LANES, LANES), 0)
    acrossf = across.astype(F32)
    slotf = (across % CAP).astype(F32)
    for i in range(CHUNKS):
        shape = (LANES, 3 * LANES)
        chosen = ones_where(iota(shape, 0) == i + CHUNKS * (iota(shape, 1) // LANES))
        wide = dot(columns, chosen)
        owner, rank, live = (wide[:, s * LANES : (s + 1) * LANES] for s in range(3))
        here = slice(i * LANES, (i + 1) * LANES)
        hot[here, :] = ones_where(owner == acrossf)
        slots[here, :] = ones_where(slotf == rank)
        alive[here, :] = jnp.where(acrossf < live, 1.0, 0.0)
        turned[:, here] = ones_where(down == owner_ref[i : i + 1, :])
    shape = (PIECES * LANES, NVAR * LANES)
    spread[...] = ones_where((iota(shape, 0) % LANES) // CAP == iota(shape, 1) // LANES)

    answers = jnp.concatenate(split(ans_ref[...]), axis=1)
    received = dot(hot[...], answers).astype(BF16)
    gas_wide[...] = dot(received * jnp.concatenate([slots[...]] * PIECES, axis=1), spread[...])
    kind = iota((PART, LANES), 1) // CAP
    stores = []
    for part in range(parts):
        here = slice(part * PART, (part + 1) * PART)
        slot = slots[here, :]
        gas_vars = [gas_wide[here, c * LANES : (c + 1) * LANES] for c in range(NVAR)]
        fetches[part].wait()
        old = [held[c, here, :] for c in range(5)]
        living = alive[here, :] > 0.0
        new = [jnp.where(living, n, o) for n, o in zip(integrate(old, gas_vars), old)]
        for c in range(5):
            made[c, here, :] = new[c]
        stores.append(pltpu.make_async_copy(made.at[:, here, :], new_ref.at[:, here, :], sent.at[part]))
        stores[part].start()
    for part in range(parts):
        here = slice(part * PART, (part + 1) * PART)
        slot = slots[here, :]
        old = [held[c, here, :] for c in range(5)]
        new = [made[c, here, :] for c in range(5)]
        change = [old[0] - new[0]] + [old[0] * old[c] - new[0] * new[c] for c in range(1, 5)]
        total = jnp.zeros((PART, LANES), F32)
        for c in range(NVAR):
            total = jnp.where(kind == c, jnp.sum(change[c], axis=1, keepdims=True), total)
        for p, piece in enumerate(split(total)):
            placed[here, p * LANES : (p + 1) * LANES] = piece * slot
    send = dot(turned[...], placed[...])
    outgoing[...] = sum(send[:, p * LANES : (p + 1) * LANES] for p in range(PIECES))
    post = pltpu.make_async_copy(outgoing, send_ref, posted)
    post.start()
    for store in stores:
        store.wait()
    post.wait()


def scatter_kernel(asked_ref, come_ref, section_ref, out_ref, total, made, sent):
    row, lane = cell_parts(asked_ref)
    pieces = [p.astype(F32) for p in split(come_ref[...].T)]
    for start in range(0, CAP, SCATTERED):
        hots, parts = [], []
        for k in range(start, start + SCATTERED):
            hot = ones_where(iota((2 * ROWS, LANES), 0) == row[k : k + 1])
            here = iota((LANES, LANES), 0) == lane[k : k + 1]
            for piece in pieces:
                hots.append(hot)
                parts.append(
                    jnp.concatenate(
                        [
                            jnp.where(here, piece[c * CAP + k : c * CAP + k + 1], 0.0)
                            for c in range(NVAR)
                        ],
                        axis=0,
                    ).astype(BF16)
                )
        added = dot_nt(jnp.concatenate(parts, axis=1), jnp.concatenate(hots, axis=1))
        if start == 0:
            total[...] = added
        else:
            total[...] += added
    copies = []

    def send(c):
        copies.append(pltpu.make_async_copy(made.at[c], out_ref.at[c], sent.at[c]))
        copies[-1].start()

    for c in range(NVAR):
        for half in range(2):
            cells = WEIGHT * total[c * LANES : (c + 1) * LANES, half * ROWS : (half + 1) * ROWS].T
            z = slice(half * LANES, (half + 1) * LANES)
            made[c, :, z] = section_ref[c, :, z] + cells
            if c == 0:
                made[NVAR, :, z] = section_ref[NVAR, :, z] + cells
        send(c)
        if c == 0:
            send(NVAR)
    for copy in copies:
        copy.wait()


def gas_kernel(gas_ref, edge_ref, below, above, low, high, out_ref, q0, q1, q2, prim, face):
    place, pair = lax.axis_index("gas"), lax.axis_index("grp")
    own = pl.ds(pl.multiple_of(pair * 8, 8), CY)
    side = pl.ds(pl.multiple_of((1 - pair) * CY, 8), 8)
    inner = slice(HALO, HALO + CX)
    q0[:, inner, own, :] = gas_ref[...]
    q0[:, inner, side, :] = edge_ref[...]
    at_corner = FAR * CY

    def rows_beside(pair, below_ref, above_ref):
        mine = slice(8 * pair, 8 * pair + CY)
        q0[:, HALO - 1, mine, :] = below_ref[...]
        q0[:, HALO + CX, mine, :] = above_ref[...]

    def rows_beyond(pair, low_ref, high_ref):
        mine = slice(8 * pair, 8 * pair + CY)
        near, after = ((CY, CY + 1), (7, 6))[pair]
        for i in range(FAR):
            q0[:, i, mine, :] = low_ref[:, i * CY : (i + 1) * CY, :]
            q0[:, HALO + CX + 1 + i, mine, :] = high_ref[:, i * CY : (i + 1) * CY, :]
        for ref, one, two in ((low_ref, HALO - 1, HALO - 2), (high_ref, HALO + CX, HALO + CX + 1)):
            q0[:, one, near : near + 1, :] = ref[:, at_corner : at_corner + 1, :]
            q0[:, one, after : after + 1, :] = ref[:, at_corner + 1 : at_corner + 2, :]
            q0[:, two, near : near + 1, :] = ref[:, at_corner + 2 : at_corner + 3, :]

    by_core(rows_beside, below, above)
    by_core(rows_beyond, low, high)

    def ghosts(q):
        @pl.when(place == 0)
        def _():
            q[:, HALO - 1] = q[:, HALO]

        @pl.when(place == lax.axis_size("gas") - 1)
        def _():
            q[:, HALO + CX] = q[:, HALO + CX - 1]

    tiles, halves = EXT_Y // 8, range(NZ // LANES)
    row_in_tile, lane = iota((8, LANES), 0), iota((8, LANES), 1)

    def at(ref, c, x, t):
        return [ref[c, x, 8 * t : 8 * t + 8, h * LANES : (h + 1) * LANES] for h in halves]

    def each(f, *lists):
        return [f(*items) for items in zip(*lists)]

    def y_turned(v):
        return [pltpu.roll(part, 7, 0) for part in v]

    def y_above(v, turned, turned_next):
        after = v if turned_next is None else turned_next
        return each(lambda m, n: jnp.where(row_in_tile == 7, n, m), turned, after)

    def z_above(v):
        left, right = (pltpu.roll(part, LANES - 1, 1) for part in v)
        return [jnp.where(lane == LANES - 1, right, left), jnp.where(lane == LANES - 1, v[1], right)]

    def z_below(g, first):
        left, right = (pltpu.roll(part, 1, 1) for part in g)
        return [jnp.where(lane == 0, first, left), jnp.where(lane == 0, left, right)]

    def weights(u, sound, un, soundn):
        rate = each(lambda u, s, un, sn: jnp.maximum(jnp.abs(u) + s, jnp.abs(un) + sn), u, sound, un, soundn)
        return each(jnp.add, u, rate), each(jnp.subtract, un, rate)

    def face_flux(v, here, vn, there, p=None, pn=None):
        g = each(lambda v, w, vn, wn: v * w + vn * wn, v, here, vn, there)
        return g if p is None else each(lambda g, p, pn: g + (p + pn), g, p, pn)

    def primitives(q, x):
        inverse = 1.0 / q[0, x]
        for d in range(3):
            prim[d, x] = q[1 + d, x] * inverse
        prim[3, x] = jnp.sqrt(GAMMA_ADIABATIC * (q[4, x] * inverse))

    def x_faces(q, x, t):
        here, there = weights(at(prim, 0, x, t), at(prim, 3, x, t), at(prim, 0, x + 1, t), at(prim, 3, x + 1, t))
        faces = []
        for c in range(6):
            pressure = (at(q, 4, x, t), at(q, 4, x + 1, t)) if c == 1 else ()
            faces.append(face_flux(at(q, c, x, t), here, at(q, c, x + 1, t), there, *pressure))
        return faces

    def update(q, combine, start, stop):
        def fill(x, carry):
            primitives(q, x)
            return carry

        lax.fori_loop(start - 1, stop + 1, fill, 0, unroll=2)
        for t in range(tiles):
            for c, value in enumerate(x_faces(q, start - 1, t)):
                for h in halves:
                    face[c, 8 * t : 8 * t + 8, h * LANES : (h + 1) * LANES] = value[h]

        def row(x, carry):
            turned = [y_turned(at(q, c, x, 0)) for c in range(6)]
            turned_u, turned_s = y_turned(at(prim, 1, x, 0)), y_turned(at(prim, 3, x, 0))
            shifted = [None] * 6
            for t in range(tiles):
                rows = slice(8 * t, 8 * t + 8)
                final = t == tiles - 1
                v = [at(q, c, x, t) for c in range(6)]
                sound = at(prim, 3, x, t)

                change = []
                for c, upper in enumerate(x_faces(q, x, t)):
                    z = [slice(h * LANES, (h + 1) * LANES) for h in halves]
                    change.append([upper[h] - face[c, rows, z[h]] for h in halves])
                    for h in halves:
                        face[c, rows, z[h]] = upper[h]

                u = at(prim, 1, x, t)
                next_u = None if final else y_turned(at(prim, 1, x, t + 1))
                next_s = None if final else y_turned(at(prim, 3, x, t + 1))
                here, there = weights(u, sound, y_above(u, turned_u, next_u), y_above(sound, turned_s, next_s))
                turned_u, turned_s = next_u, next_s
                next_v = [None if final else y_turned(at(q, c, x, t + 1)) for c in range(6)]
                above = [y_above(v[c], turned[c], next_v[c]) for c in range(6)]
                turned = next_v
                for c in range(6):
                    pressure = (v[4], above[4]) if c == 2 else ()
                    g = face_flux(v[c], here, above[c], there, *pressure)
                    moved = [pltpu.roll(part, 1, 0) for part in g]
                    if t == 0:
                        first = each(lambda v, u: 2.0 * (v * u), v[c], u)
                        if c == 2:
                            first = each(lambda f, p: f + 2.0 * p, first, v[4])
                    else:
                        first = shifted[c]
                    below = each(lambda f, m: jnp.where(row_in_tile == 0, f, m), first, moved)
                    shifted[c] = moved
                    change[c] = each(lambda k, g, b: k + (g - b), change[c], g, below)

                u = at(prim, 2, x, t)
                here, there = weights(u, sound, z_above(u), z_above(sound))
                above_p = z_above(v[4])
                for c in range(6):
                    above_v = above_p if c == 4 else z_above(v[c])
                    pressure = (v[4], above_p) if c == 3 else ()
                    g = face_flux(v[c], here, above_v, there, *pressure)
                    first = 2.0 * (v[c][0] * u[0])
                    if c == 3:
                        first = first + 2.0 * v[4][0]
                    below = z_below(g, first)
                    change[c] = each(lambda k, g, b: k + (g - b), change[c], g, below)

                for c in range(6):
                    for h in halves:
                        z = slice(h * LANES, (h + 1) * LANES)
                        combine(c, x, rows, z, v[c][h] - (0.5 * LAM) * change[c][h])
            return carry

        lax.fori_loop(start, stop, row, 0)

    ghosts(q0)

    def first_section(c, x, rows, z, value):
        q1[c, x, rows, z] = value

    update(q0, first_section, 1, EXT_X - 1)
    ghosts(q1)

    def second_section(c, x, rows, z, value):
        q2[c, x, rows, z] = 0.75 * q0[c, x, rows, z] + 0.25 * value

    update(q1, second_section, 2, EXT_X - 2)
    ghosts(q2)

    def third_section(c, x, rows, z, value):
        q1[c, x, rows, z] = q0[c, x, rows, z] * (1.0 / 3.0) + (2.0 / 3.0) * value

    update(q2, third_section, HALO, HALO + CX)
    out_ref[...] = q1[:, inner, own, :]


LARGE_FLOPS = 10**9
LARGE = pl.CostEstimate(flops=LARGE_FLOPS, bytes_accessed=1, transcendentals=0)
SMALL = pl.CostEstimate(flops=1, bytes_accessed=1, transcendentals=0)


def call(kernel, mib, outs, scratch=(), cost=SMALL, **more):
    return pl.pallas_call(
        kernel,
        out_shape=outs,
        scratch_shapes=list(scratch),
        compiler_params=compiler_params(mib),
        cost_estimate=cost,
        **more,
    )


def deliver(buffer):
    return lax.all_to_all(buffer, AXES, split_axis=0, concat_axis=0, tiled=True)


HELD = pl.BlockSpec(memory_space=pltpu.VMEM)
ANYWHERE = pl.BlockSpec(memory_space=pl.ANY)


def in_hbm(array):
    return pltpu.with_memory_space_constraint(array, pltpu.HBM)


def integrate_parcels(owner, rank, live, answered, parcels):
    return call(
        parcel_kernel,
        24,
        [
            jax.ShapeDtypeStruct((5, BLK_DEV, LANES), F32),
            jax.ShapeDtypeStruct((DEVICES, LANES), F32),
        ],
        [
            pltpu.VMEM((5, BLK_DEV, LANES), F32),
            pltpu.VMEM((5, BLK_DEV, LANES), F32),
            pltpu.VMEM((BLK_DEV, DEVICES), BF16),
            pltpu.VMEM((DEVICES, BLK_DEV), BF16),
            pltpu.VMEM((BLK_DEV, LANES), BF16),
            pltpu.VMEM((BLK_DEV, LANES), F32),
            pltpu.VMEM((PIECES * LANES, NVAR * LANES), BF16),
            pltpu.VMEM((BLK_DEV, PIECES * LANES), BF16),
            pltpu.VMEM((DEVICES, LANES), F32),
            pltpu.VMEM((BLK_DEV, NVAR * LANES), F32),
            pltpu.SemaphoreType.DMA((BLK_DEV // PART,)),
            pltpu.SemaphoreType.DMA((BLK_DEV // PART,)),
            pltpu.SemaphoreType.DMA,
        ],
        cost=pl.CostEstimate(flops=PARCEL_FLOPS, bytes_accessed=8 * 5 * BLK_DEV * LANES, transcendentals=0),
        in_specs=[HELD] * 4 + [ANYWHERE],
        out_specs=[ANYWHERE, ANYWHERE],
    )(owner, rank, live, answered, in_hbm(parcels))


def body(gas_state, particle_blocks, owner, host_cell, live_count):
    pair = lax.axis_index("grp")
    count = lax.axis_size("gas")
    owner = owner.reshape(CHUNKS, LANES)
    host_cell = host_cell.reshape(CHUNKS, LANES)
    live = live_count.reshape(CHUNKS, LANES)
    square = jax.ShapeDtypeStruct((DEVICES, LANES), F32)

    requests, rank = call(
        request_kernel,
        8,
        [
            jax.ShapeDtypeStruct((DEVICES, LANES), jnp.int32),
            jax.ShapeDtypeStruct((CHUNKS, LANES), jnp.int32),
        ],
    )(in_hbm(owner), in_hbm(host_cell))
    asked = deliver(requests)

    mine, _ = lax.optimization_barrier((gas_state, requests))
    circuit = [(i, (i + 1) % count) for i in range(count)]
    back = [(target, source) for source, target in circuit]
    row = jax.ShapeDtypeStruct((6, CY, NZ), F32)
    table, first, second, edge = call(
        table_kernel,
        12,
        [
            jax.ShapeDtypeStruct((NVAR * LANES, PIECES * 2 * ROWS), BF16),
            row,
            row,
            jax.ShapeDtypeStruct((6, CX, 8, NZ), F32),
        ],
    )(mine)
    edge = lax.ppermute(edge, "grp", [(0, 1), (1, 0)])
    below = lax.ppermute(first, "gas", circuit)
    above = lax.ppermute(second, "gas", back)
    replies = call(gather_kernel, 16, square, [pltpu.VMEM((LANES, LANES), F32)], cost=LARGE)(asked, table)
    answered = deliver(replies)

    edge, below, above, replies = lax.optimization_barrier(
        (edge, below, above, replies)
    )
    message = jax.ShapeDtypeStruct((6, FAR * CY + 8, NZ), F32)
    first, second = call(message_kernel, 12, [message, message])(gas_state, edge)
    low = lax.ppermute(first, "gas", circuit)
    high = lax.ppermute(second, "gas", back)
    parcels_next, sources = integrate_parcels(owner, rank, live, answered, particle_blocks)
    come = deliver(sources)

    below, above, low, high, _ = lax.optimization_barrier(
        (below, above, low, high, sources)
    )
    extended = pltpu.VMEM((6, EXT_X, EXT_Y, NZ), F32)
    section_three = call(
        gas_kernel,
        28,
        jax.ShapeDtypeStruct((6, CX, CY, NZ), F32),
        [
            extended,
            extended,
            extended,
            pltpu.VMEM((4, EXT_X, EXT_Y, NZ), F32),
            pltpu.VMEM((6, EXT_Y, NZ), F32),
        ],
    )(gas_state, edge, below, above, low, high)

    gas_next = call(
        scatter_kernel,
        20,
        jax.ShapeDtypeStruct((6, ROWS, NZ), F32),
        [
            pltpu.VMEM((NVAR * LANES, 2 * ROWS), F32),
            pltpu.VMEM((6, ROWS, NZ), F32),
            pltpu.SemaphoreType.DMA((6,)),
        ],
        out_specs=ANYWHERE,
    )(asked, come, section_three.reshape(6, ROWS, NZ))
    return (gas_next.reshape(6, CX, CY, NZ), parcels_next)


def solution(mesh):
    placed = (
        P(None, "gas", "grp", None),
        P(None, AXES, None),
        P(AXES, None),
        P(AXES),
        P(AXES),
    )
    return jax.shard_map(
        body,
        mesh=mesh,
        in_specs=placed,
        out_specs=(P(None, "gas", "grp", None), P(None, AXES, None)),
        check_vma=False,
    )
```

```python
import jax
import jax.numpy as jnp
from jax import lax
from jax.experimental import pallas as pl
from jax.experimental.pallas import tpu as pltpu
from jax.sharding import PartitionSpec as P

AXES = ("gas", "grp")
DEVICES = 128
LANES = 128
CAP = 16
CX, CY, NZ = 4, 32, 256
ROWS = CX * CY
BLK_DEV = 1024
CHUNKS = BLK_DEV // LANES
NSUB = 4
NVAR = 5
PIECES = 2
HALO = 3
FAR = HALO - 1
PART = 256
GATHERED = 2
SCATTERED = 2
PARCEL_FLOPS = 10**10
EXT_X = CX + 2 * HALO
EXT_Y = CY + 8

LAM = 0.1
GAMMA_ADIABATIC = 1.4
CLOCK_INCREMENT = 0.25
TAU_DRAG = 0.8
THERMAL_RELAX = 1.2
EVAP_RATE = 0.5
LATENT_EVAPORATE = 0.3
WEIGHT = 0.05
LOG2E = 1.4426950408889634

F32 = jnp.float32
BF16 = jnp.bfloat16
MIB = 1024 * 1024


def iota(shape, dim):
    return lax.broadcasted_iota(jnp.int32, shape, dim)


def dot(a, b):
    return lax.dot_general(a, b, (((1,), (0,)), ((), ())), preferred_element_type=F32)


def dot_nt(a, b):
    return lax.dot_general(a, b, (((1,), (1,)), ((), ())), preferred_element_type=F32)


def split(x):
    pieces = []
    for _ in range(PIECES):
        piece = x.astype(BF16)
        pieces.append(piece)
        x = x - piece.astype(F32)
    return pieces


def ones_where(mask):
    return jnp.where(mask, 1.0, 0.0).astype(BF16)


def compiler_params(mib):
    return pltpu.CompilerParams(vmem_limit_bytes=mib * MIB)


def request_kernel(owner_ref, cell_ref, req_ref, rank_ref):
    down = iota((LANES, LANES), 0)
    across = iota((LANES, 2 * LANES), 1)
    earlier = ones_where((iota((LANES, 2 * LANES), 0) < across) | (across >= LANES))
    named = [down == owner_ref[i : i + 1, :] for i in range(CHUNKS)]
    hots = [ones_where(n) for n in named]
    counts = dot(jnp.concatenate(hots, axis=0), earlier)
    before = jnp.zeros((LANES, LANES), F32)
    slots = iota((CAP, LANES), 0)
    highs, lows = [], []
    for i in range(CHUNKS):
        count = counts[i * LANES : (i + 1) * LANES]
        place = jnp.where(named[i], count[:, :LANES] + before, 0.0)
        rank = jnp.sum(place, axis=0, keepdims=True).astype(jnp.int32)
        rank_ref[i : i + 1, :] = rank
        before = before + count[:, LANES:]
        cell = cell_ref[i : i + 1, :]
        placed = slots == rank
        highs.append(jnp.where(placed, (((cell >> 8) + 1) << 8).astype(F32), 0.0))
        lows.append(jnp.where(placed, (cell & 255).astype(F32), 0.0))
    values = jnp.concatenate(highs + lows, axis=1).astype(BF16)
    total = dot_nt(jnp.concatenate(hots + hots, axis=1), values)
    req_ref[...] = jnp.full((DEVICES, LANES), -1, jnp.int32)
    req_ref[:, :CAP] = total.astype(jnp.int32) - 256


def by_core(action, *refs):
    pair = lax.axis_index("grp")
    for core in range(2):
        pl.when(pair == core)(lambda: action(core, *refs))


def table_kernel(gas_ref, table_ref, up_ref, down_ref, edge_ref):
    up_ref[...] = gas_ref[:, CX - 1]
    down_ref[...] = gas_ref[:, 0]

    def beside(pair):
        start = (1 - pair) * (CY - 8)
        edge_ref[...] = gas_ref[:, :, start : start + 8]

    by_core(beside)
    inverse = 1.0 / gas_ref[0].reshape(ROWS, NZ)
    for c in range(NVAR):
        value = gas_ref[1 + c].reshape(ROWS, NZ) * inverse
        for half in range(2):
            turned = value[:, half * LANES : (half + 1) * LANES].T
            for p, piece in enumerate(split(turned)):
                start = p * 2 * ROWS + half * ROWS
                table_ref[c * LANES : (c + 1) * LANES, start : start + ROWS] = piece


def message_kernel(gas_ref, edge_ref, first_ref, second_ref):
    at = FAR * CY

    def fill(pair, up_ref, down_ref):
        near, after = ((0, 1), (7, 6))[pair]
        for i in range(FAR):
            here = slice(i * CY, (i + 1) * CY)
            up_ref[:, here, :] = gas_ref[:, CX - HALO + i]
            down_ref[:, here, :] = gas_ref[:, 1 + i]
        for ref, one, two in ((up_ref, CX - 1, CX - 2), (down_ref, 0, 1)):
            ref[:, at : at + 8, :] = jnp.zeros((6, 8, NZ), F32)
            ref[:, at : at + 1, :] = edge_ref[:, one, near : near + 1, :]
            ref[:, at + 1 : at + 2, :] = edge_ref[:, one, after : after + 1, :]
            ref[:, at + 2 : at + 3, :] = edge_ref[:, two, near : near + 1, :]

    by_core(fill, first_ref, second_ref)


def cell_parts(asked_ref):
    cell = asked_ref[...].astype(F32).T.astype(jnp.int32)
    return (cell >> 8) + ROWS * ((cell >> 7) & 1), cell & (LANES - 1)


def gather_kernel(asked_ref, table_ref, reply_ref, found):
    row, lane = cell_parts(asked_ref)
    table = table_ref[...]
    found[...] = jnp.zeros((LANES, LANES), F32)
    for k in range(0, CAP, GATHERED):
        rows = jnp.concatenate([row[k + j : k + j + 1] for j in range(GATHERED)], axis=1)
        lanes = jnp.concatenate([lane[k + j : k + j + 1] for j in range(GATHERED)], axis=1)
        hot = ones_where(iota((2 * ROWS, GATHERED * LANES), 0) == rows)
        values = dot(table, jnp.concatenate([hot] * PIECES, axis=0))
        here = iota((LANES, GATHERED * LANES), 0) == lanes
        for c in range(NVAR):
            part = values[c * LANES : (c + 1) * LANES]
            picked = jnp.sum(jnp.where(here, part, 0.0), axis=0, keepdims=True)
            for j in range(GATHERED):
                at = c * CAP + k + j
                found[at : at + 1, :] = picked[:, j * LANES : (j + 1) * LANES]
    reply_ref[...] = found[...].T


def integrate(parcels, gas_vars):
    mass, speeds, thermal = parcels[0], parcels[1:4], parcels[4]
    ambient, vapor = gas_vars[3], gas_vars[4]
    power = first_power = (-2.0 / 3.0) * jnp.log2(mass)
    exposure = None
    rate = CLOCK_INCREMENT * EVAP_RATE * LOG2E
    headroom = rate * (0.3 - vapor)
    offset = ambient + LATENT_EVAPORATE
    for _ in range(NSUB):
        inverse = jnp.exp2(power)
        square = 1.0 + thermal * thermal
        guess = pl.reciprocal(square, approx=True)
        guess = guess * (2.0 - square * guess)
        loss = (headroom - (0.3 * rate) * guess) * inverse
        kept = jnp.exp2((-CLOCK_INCREMENT / THERMAL_RELAX * LOG2E) * inverse)
        thermal = offset + (thermal - ambient) * kept - LATENT_EVAPORATE * jnp.exp2(loss)
        power = power + (2.0 / 3.0) * loss
        exposure = inverse if exposure is None else exposure + inverse
    drag = jnp.exp2((-CLOCK_INCREMENT / TAU_DRAG * LOG2E) * exposure)
    moved = [gas_vars[c] + (speeds[c] - gas_vars[c]) * drag for c in range(3)]
    return [mass * jnp.exp2(1.5 * (first_power - power))] + moved + [thermal]


def prepare_kernel(owner_ref, rank_ref, live_ref, hot_ref, turned_ref, code_ref):
    pad = jnp.zeros((LANES - 3 * CHUNKS, LANES), F32)
    rows = [owner_ref[...], rank_ref[...], live_ref[...]]
    stack = jnp.concatenate([r.astype(F32) for r in rows] + [pad], axis=0)
    columns = stack.T.astype(BF16)
    across, down = iota((LANES, LANES), 1), iota((LANES, LANES), 0)
    lane = across.astype(F32)
    lane_slot = (across % CAP).astype(F32)
    for i in range(CHUNKS):
        shape = (LANES, 3 * LANES)
        chosen = ones_where(iota(shape, 0) == i + CHUNKS * (iota(shape, 1) // LANES))
        wide = dot(columns, chosen)
        owner, rank, live = (wide[:, s * LANES : (s + 1) * LANES] for s in range(3))
        here = slice(i * LANES, (i + 1) * LANES)
        hot_ref[here, :] = ones_where(owner == lane)
        code = jnp.where(lane_slot == rank, 1.0, 0.0) + jnp.where(lane < live, 2.0, 0.0)
        code_ref[here, :] = code.astype(BF16)
        turned_ref[:, here] = ones_where(down == owner_ref[i : i + 1, :])


def parcel_kernel(
    ans_ref, hot_ref, turned_ref, code_ref, old_ref, new_ref, send_ref,
    held, made, spread, placed, outgoing, gas_wide, got, sent, posted,
):
    parts = BLK_DEV // PART
    fetches = []
    for part in range(parts):
        here = slice(part * PART, (part + 1) * PART)
        fetches.append(pltpu.make_async_copy(old_ref.at[:, here, :], held.at[:, here, :], got.at[part]))
        fetches[part].start()

    shape = (PIECES * LANES, NVAR * LANES)
    spread[...] = ones_where((iota(shape, 0) % LANES) // CAP == iota(shape, 1) // LANES)

    answers = jnp.concatenate(split(ans_ref[...]), axis=1)
    code = code_ref[...].astype(F32)
    slots = jnp.where(code > 1.5, code - 2.0, code).astype(BF16)
    received = dot(hot_ref[...], answers).astype(BF16)
    gas_wide[...] = dot(received * jnp.concatenate([slots] * PIECES, axis=1), spread[...])
    kind = iota((PART, LANES), 1) // CAP
    stores = []
    for part in range(parts):
        here = slice(part * PART, (part + 1) * PART)
        slot = slots[here]
        gas_vars = [gas_wide[here, c * LANES : (c + 1) * LANES] for c in range(NVAR)]
        fetches[part].wait()
        old = [held[c, here, :] for c in range(5)]
        living = code_ref[here, :].astype(F32) > 1.5
        new = [jnp.where(living, n, o) for n, o in zip(integrate(old, gas_vars), old)]
        for c in range(5):
            made[c, here, :] = new[c]
        stores.append(pltpu.make_async_copy(made.at[:, here, :], new_ref.at[:, here, :], sent.at[part]))
        stores[part].start()
    for part in range(parts):
        here = slice(part * PART, (part + 1) * PART)
        slot = slots[here]
        old = [held[c, here, :] for c in range(5)]
        new = [made[c, here, :] for c in range(5)]
        change = [old[0] - new[0]] + [old[0] * old[c] - new[0] * new[c] for c in range(1, 5)]
        total = jnp.zeros((PART, LANES), F32)
        for c in range(NVAR):
            total = jnp.where(kind == c, jnp.sum(change[c], axis=1, keepdims=True), total)
        for p, piece in enumerate(split(total)):
            placed[here, p * LANES : (p + 1) * LANES] = piece * slot
    send = dot(turned_ref[...], placed[...])
    outgoing[...] = sum(send[:, p * LANES : (p + 1) * LANES] for p in range(PIECES))
    post = pltpu.make_async_copy(outgoing, send_ref, posted)
    post.start()
    for store in stores:
        store.wait()
    post.wait()


def scatter_kernel(asked_ref, come_ref, section_ref, out_ref, total, made, sent):
    row, lane = cell_parts(asked_ref)
    pieces = [p.astype(F32) for p in split(come_ref[...].T)]
    for start in range(0, CAP, SCATTERED):
        hots, parts = [], []
        for k in range(start, start + SCATTERED):
            hot = ones_where(iota((2 * ROWS, LANES), 0) == row[k : k + 1])
            here = iota((LANES, LANES), 0) == lane[k : k + 1]
            for piece in pieces:
                hots.append(hot)
                parts.append(
                    jnp.concatenate(
                        [
                            jnp.where(here, piece[c * CAP + k : c * CAP + k + 1], 0.0)
                            for c in range(NVAR)
                        ],
                        axis=0,
                    ).astype(BF16)
                )
        added = dot_nt(jnp.concatenate(parts, axis=1), jnp.concatenate(hots, axis=1))
        if start == 0:
            total[...] = added
        else:
            total[...] += added
    copies = []

    def send(c):
        copies.append(pltpu.make_async_copy(made.at[c], out_ref.at[c], sent.at[c]))
        copies[-1].start()

    for c in range(NVAR):
        for half in range(2):
            cells = WEIGHT * total[c * LANES : (c + 1) * LANES, half * ROWS : (half + 1) * ROWS].T
            z = slice(half * LANES, (half + 1) * LANES)
            made[c, :, z] = section_ref[c, :, z] + cells
            if c == 0:
                made[NVAR, :, z] = section_ref[NVAR, :, z] + cells
        send(c)
        if c == 0:
            send(NVAR)
    for copy in copies:
        copy.wait()


def gas_kernel(gas_ref, edge_ref, below, above, low, high, out_ref, q0, q1, q2, prim, face):
    place, pair = lax.axis_index("gas"), lax.axis_index("grp")
    own = pl.ds(pl.multiple_of(pair * 8, 8), CY)
    side = pl.ds(pl.multiple_of((1 - pair) * CY, 8), 8)
    inner = slice(HALO, HALO + CX)
    q0[:, inner, own, :] = gas_ref[...]
    q0[:, inner, side, :] = edge_ref[...]
    at_corner = FAR * CY

    def rows_beside(pair, below_ref, above_ref):
        mine = slice(8 * pair, 8 * pair + CY)
        q0[:, HALO - 1, mine, :] = below_ref[...]
        q0[:, HALO + CX, mine, :] = above_ref[...]

    def rows_beyond(pair, low_ref, high_ref):
        mine = slice(8 * pair, 8 * pair + CY)
        near, after = ((CY, CY + 1), (7, 6))[pair]
        for i in range(FAR):
            q0[:, i, mine, :] = low_ref[:, i * CY : (i + 1) * CY, :]
            q0[:, HALO + CX + 1 + i, mine, :] = high_ref[:, i * CY : (i + 1) * CY, :]
        for ref, one, two in ((low_ref, HALO - 1, HALO - 2), (high_ref, HALO + CX, HALO + CX + 1)):
            q0[:, one, near : near + 1, :] = ref[:, at_corner : at_corner + 1, :]
            q0[:, one, after : after + 1, :] = ref[:, at_corner + 1 : at_corner + 2, :]
            q0[:, two, near : near + 1, :] = ref[:, at_corner + 2 : at_corner + 3, :]

    by_core(rows_beside, below, above)
    by_core(rows_beyond, low, high)

    def ghosts(q):
        @pl.when(place == 0)
        def _():
            q[:, HALO - 1] = q[:, HALO]

        @pl.when(place == lax.axis_size("gas") - 1)
        def _():
            q[:, HALO + CX] = q[:, HALO + CX - 1]

    tiles, halves = EXT_Y // 8, range(NZ // LANES)
    row_in_tile, lane = iota((8, LANES), 0), iota((8, LANES), 1)

    def at(ref, c, x, t):
        return [ref[c, x, 8 * t : 8 * t + 8, h * LANES : (h + 1) * LANES] for h in halves]

    def each(f, *lists):
        return [f(*items) for items in zip(*lists)]

    def y_turned(v):
        return [pltpu.roll(part, 7, 0) for part in v]

    def y_above(v, turned, turned_next):
        after = v if turned_next is None else turned_next
        return each(lambda m, n: jnp.where(row_in_tile == 7, n, m), turned, after)

    def z_above(v):
        left, right = (pltpu.roll(part, LANES - 1, 1) for part in v)
        return [jnp.where(lane == LANES - 1, right, left), jnp.where(lane == LANES - 1, v[1], right)]

    def z_below(g, first):
        left, right = (pltpu.roll(part, 1, 1) for part in g)
        return [jnp.where(lane == 0, first, left), jnp.where(lane == 0, left, right)]

    def weights(u, sound, un, soundn):
        rate = each(lambda u, s, un, sn: jnp.maximum(jnp.abs(u) + s, jnp.abs(un) + sn), u, sound, un, soundn)
        return each(jnp.add, u, rate), each(jnp.subtract, un, rate)

    def face_flux(v, here, vn, there, p=None, pn=None):
        g = each(lambda v, w, vn, wn: v * w + vn * wn, v, here, vn, there)
        return g if p is None else each(lambda g, p, pn: g + (p + pn), g, p, pn)

    def primitives(q, x):
        inverse = 1.0 / q[0, x]
        for d in range(3):
            prim[d, x] = q[1 + d, x] * inverse
        prim[3, x] = jnp.sqrt(GAMMA_ADIABATIC * (q[4, x] * inverse))

    def x_faces(q, x, t):
        here, there = weights(at(prim, 0, x, t), at(prim, 3, x, t), at(prim, 0, x + 1, t), at(prim, 3, x + 1, t))
        faces = []
        for c in range(6):
            pressure = (at(q, 4, x, t), at(q, 4, x + 1, t)) if c == 1 else ()
            faces.append(face_flux(at(q, c, x, t), here, at(q, c, x + 1, t), there, *pressure))
        return faces

    def update(q, combine, start, stop):
        def fill(x, carry):
            primitives(q, x)
            return carry

        lax.fori_loop(start - 1, stop + 1, fill, 0, unroll=2)
        for t in range(tiles):
            for c, value in enumerate(x_faces(q, start - 1, t)):
                for h in halves:
                    face[c, 8 * t : 8 * t + 8, h * LANES : (h + 1) * LANES] = value[h]

        def row(x, carry):
            turned = [y_turned(at(q, c, x, 0)) for c in range(6)]
            turned_u, turned_s = y_turned(at(prim, 1, x, 0)), y_turned(at(prim, 3, x, 0))
            shifted = [None] * 6
            for t in range(tiles):
                rows = slice(8 * t, 8 * t + 8)
                final = t == tiles - 1
                v = [at(q, c, x, t) for c in range(6)]
                sound = at(prim, 3, x, t)

                change = []
                for c, upper in enumerate(x_faces(q, x, t)):
                    z = [slice(h * LANES, (h + 1) * LANES) for h in halves]
                    change.append([upper[h] - face[c, rows, z[h]] for h in halves])
                    for h in halves:
                        face[c, rows, z[h]] = upper[h]

                u = at(prim, 1, x, t)
                next_u = None if final else y_turned(at(prim, 1, x, t + 1))
                next_s = None if final else y_turned(at(prim, 3, x, t + 1))
                here, there = weights(u, sound, y_above(u, turned_u, next_u), y_above(sound, turned_s, next_s))
                turned_u, turned_s = next_u, next_s
                next_v = [None if final else y_turned(at(q, c, x, t + 1)) for c in range(6)]
                above = [y_above(v[c], turned[c], next_v[c]) for c in range(6)]
                turned = next_v
                for c in range(6):
                    pressure = (v[4], above[4]) if c == 2 else ()
                    g = face_flux(v[c], here, above[c], there, *pressure)
                    moved = [pltpu.roll(part, 1, 0) for part in g]
                    if t == 0:
                        first = each(lambda v, u: 2.0 * (v * u), v[c], u)
                        if c == 2:
                            first = each(lambda f, p: f + 2.0 * p, first, v[4])
                    else:
                        first = shifted[c]
                    below = each(lambda f, m: jnp.where(row_in_tile == 0, f, m), first, moved)
                    shifted[c] = moved
                    change[c] = each(lambda k, g, b: k + (g - b), change[c], g, below)

                u = at(prim, 2, x, t)
                here, there = weights(u, sound, z_above(u), z_above(sound))
                above_p = z_above(v[4])
                for c in range(6):
                    above_v = above_p if c == 4 else z_above(v[c])
                    pressure = (v[4], above_p) if c == 3 else ()
                    g = face_flux(v[c], here, above_v, there, *pressure)
                    first = 2.0 * (v[c][0] * u[0])
                    if c == 3:
                        first = first + 2.0 * v[4][0]
                    below = z_below(g, first)
                    change[c] = each(lambda k, g, b: k + (g - b), change[c], g, below)

                for c in range(6):
                    for h in halves:
                        z = slice(h * LANES, (h + 1) * LANES)
                        combine(c, x, rows, z, v[c][h] - (0.5 * LAM) * change[c][h])
            return carry

        lax.fori_loop(start, stop, row, 0)

    ghosts(q0)

    def first_section(c, x, rows, z, value):
        q1[c, x, rows, z] = value

    update(q0, first_section, 1, EXT_X - 1)
    ghosts(q1)

    def second_section(c, x, rows, z, value):
        q2[c, x, rows, z] = 0.75 * q0[c, x, rows, z] + 0.25 * value

    update(q1, second_section, 2, EXT_X - 2)
    ghosts(q2)

    def third_section(c, x, rows, z, value):
        q1[c, x, rows, z] = q0[c, x, rows, z] * (1.0 / 3.0) + (2.0 / 3.0) * value

    update(q2, third_section, HALO, HALO + CX)
    out_ref[...] = q1[:, inner, own, :]


LARGE_FLOPS = 10**9
LARGE = pl.CostEstimate(flops=LARGE_FLOPS, bytes_accessed=1, transcendentals=0)
SMALL = pl.CostEstimate(flops=1, bytes_accessed=1, transcendentals=0)


def call(kernel, mib, outs, scratch=(), cost=SMALL, **more):
    return pl.pallas_call(
        kernel,
        out_shape=outs,
        scratch_shapes=list(scratch),
        compiler_params=compiler_params(mib),
        cost_estimate=cost,
        **more,
    )


def deliver(buffer):
    return lax.all_to_all(buffer, AXES, split_axis=0, concat_axis=0, tiled=True)


HELD = pl.BlockSpec(memory_space=pltpu.VMEM)
ANYWHERE = pl.BlockSpec(memory_space=pl.ANY)


def in_hbm(array):
    return pltpu.with_memory_space_constraint(array, pltpu.HBM)


def in_vmem(array):
    return pltpu.with_memory_space_constraint(array, pltpu.VMEM)


def prepare(owner, rank, live):
    return call(
        prepare_kernel,
        8,
        [
            pltpu.VMEM((BLK_DEV, DEVICES), BF16),
            pltpu.VMEM((DEVICES, BLK_DEV), BF16),
            pltpu.VMEM((BLK_DEV, LANES), BF16),
        ],
    )(owner, rank, live)


def integrate_parcels(answered, prepared, parcels):
    return call(
        parcel_kernel,
        24,
        [
            jax.ShapeDtypeStruct((5, BLK_DEV, LANES), F32),
            jax.ShapeDtypeStruct((DEVICES, LANES), F32),
        ],
        [
            pltpu.VMEM((5, BLK_DEV, LANES), F32),
            pltpu.VMEM((5, BLK_DEV, LANES), F32),
            pltpu.VMEM((PIECES * LANES, NVAR * LANES), BF16),
            pltpu.VMEM((BLK_DEV, PIECES * LANES), BF16),
            pltpu.VMEM((DEVICES, LANES), F32),
            pltpu.VMEM((BLK_DEV, NVAR * LANES), F32),
            pltpu.SemaphoreType.DMA((BLK_DEV // PART,)),
            pltpu.SemaphoreType.DMA((BLK_DEV // PART,)),
            pltpu.SemaphoreType.DMA,
        ],
        cost=pl.CostEstimate(flops=PARCEL_FLOPS, bytes_accessed=8 * 5 * BLK_DEV * LANES, transcendentals=0),
        in_specs=[HELD] * 4 + [ANYWHERE],
        out_specs=[ANYWHERE, ANYWHERE],
    )(answered, *[in_vmem(p) for p in prepared], in_hbm(parcels))


def body(gas_state, particle_blocks, owner, host_cell, live_count):
    pair = lax.axis_index("grp")
    count = lax.axis_size("gas")
    owner = owner.reshape(CHUNKS, LANES)
    host_cell = host_cell.reshape(CHUNKS, LANES)
    live = live_count.reshape(CHUNKS, LANES)
    square = jax.ShapeDtypeStruct((DEVICES, LANES), F32)

    requests, rank = call(
        request_kernel,
        8,
        [
            jax.ShapeDtypeStruct((DEVICES, LANES), jnp.int32),
            jax.ShapeDtypeStruct((CHUNKS, LANES), jnp.int32),
        ],
    )(in_hbm(owner), in_hbm(host_cell))
    asked = deliver(requests)

    mine, _ = lax.optimization_barrier((gas_state, requests))
    circuit = [(i, (i + 1) % count) for i in range(count)]
    back = [(target, source) for source, target in circuit]
    row = jax.ShapeDtypeStruct((6, CY, NZ), F32)
    table, first, second, edge = call(
        table_kernel,
        12,
        [
            jax.ShapeDtypeStruct((NVAR * LANES, PIECES * 2 * ROWS), BF16),
            row,
            row,
            jax.ShapeDtypeStruct((6, CX, 8, NZ), F32),
        ],
    )(mine)
    edge = lax.ppermute(edge, "grp", [(0, 1), (1, 0)])
    below = lax.ppermute(first, "gas", circuit)
    above = lax.ppermute(second, "gas", back)
    replies = call(gather_kernel, 16, square, [pltpu.VMEM((LANES, LANES), F32)], cost=LARGE)(asked, table)
    answered = deliver(replies)

    edge, below, above, replies = lax.optimization_barrier(
        (edge, below, above, replies)
    )
    message = jax.ShapeDtypeStruct((6, FAR * CY + 8, NZ), F32)
    first, second = call(message_kernel, 12, [message, message])(gas_state, edge)
    first, rank = lax.optimization_barrier((first, rank))
    prepared = prepare(owner, rank, live)
    low = lax.ppermute(first, "gas", circuit)
    high = lax.ppermute(second, "gas", back)
    parcels_next, sources = integrate_parcels(answered, prepared, particle_blocks)
    come = deliver(sources)

    below, above, low, high, _ = lax.optimization_barrier(
        (below, above, low, high, sources)
    )
    extended = pltpu.VMEM((6, EXT_X, EXT_Y, NZ), F32)
    section_three = call(
        gas_kernel,
        28,
        jax.ShapeDtypeStruct((6, CX, CY, NZ), F32),
        [
            extended,
            extended,
            extended,
            pltpu.VMEM((4, EXT_X, EXT_Y, NZ), F32),
            pltpu.VMEM((6, EXT_Y, NZ), F32),
        ],
    )(in_hbm(gas_state), edge, below, above, low, high)

    gas_next = call(
        scatter_kernel,
        20,
        jax.ShapeDtypeStruct((6, ROWS, NZ), F32),
        [
            pltpu.VMEM((NVAR * LANES, 2 * ROWS), F32),
            pltpu.VMEM((6, ROWS, NZ), F32),
            pltpu.SemaphoreType.DMA((6,)),
        ],
        out_specs=ANYWHERE,
    )(asked, come, section_three.reshape(6, ROWS, NZ))
    return (gas_next.reshape(6, CX, CY, NZ), parcels_next)


def solution(mesh):
    placed = (
        P(None, "gas", "grp", None),
        P(None, AXES, None),
        P(AXES, None),
        P(AXES),
        P(AXES),
    )
    return jax.shard_map(
        body,
        mesh=mesh,
        in_specs=placed,
        out_specs=(P(None, "gas", "grp", None), P(None, AXES, None)),
        check_vma=False,
    )
```
